512 devices in a mesh: ctx: 16 (over z_lo, core), kvh: 8 (over x, z_hi), sess: 4 (over y).
Axes of the slice: x: 4, y: 4, z: 16 (z_hi: 2, z_lo: 8; z = z_hi * 8 + z_lo), core: 2. Of those that a mesh axis runs over, the one named last changes fastest.
Arguments:
- queries: bfloat16 [1024, 8, 16, 128], P(('sess', 'ctx'), 'kvh'), parts along dimension 0, may hold values from -64 to 64
- new_keys: bfloat16 [1024, 8, 128], P(('sess', 'ctx'), 'kvh'), parts along dimension 0, may hold values from -8 to 8
- new_values: bfloat16 [1024, 8, 128], P(('sess', 'ctx'), 'kvh'), parts along dimension 0, may hold values from -6 to 6
- cache_k: bfloat16 [32, 32768, 128], P(('sess', 'kvh'), 'ctx'), parts along dimension 0, may hold values from -4 to 4
- cache_v: bfloat16 [32, 32768, 128], P(('sess', 'kvh'), 'ctx'), parts along dimension 0, may hold values from -6 to 6
- span_bounds: int32 [16, 2], P('sess'), parts along dimension 0, may hold values from 0 to 256, as said below
- cache_len: int32 [64], P('sess'), parts along dimension 0, may hold values from 512 to 2048, as said below
- doc_start: int32 [4], P('sess'), parts along dimension 0, may hold values from 0 to 4095
Outputs:
- attended: bfloat16 [1024, 8, 16, 128], P(('sess', 'ctx'), 'kvh'), parts along dimension 0
The draws below stay inside these ranges and needn't reach their ends.
There are 4 independent parts, one for each index of `sess`. The reference program is written for one: setup_inputs(seed, part) draws one part's arguments, and reference() takes and returns one part's arrays. A program takes and returns all parts, laid end to end along the dimension named above; each array names one. Nothing has to cross between parts.
Inputs may be any that keep to these rules, and one draw needn't show every extreme that they name: `span_bounds`: span k lies within tokens k * 64 to (k + 1) * 64, and its start is below its end; spans are disjoint. `cache_len`: some shard is full in every draw.
All inputs are finite; a program needn't handle non-finite values.
Results may differ from the reference program's by a relative error of at most 0.013.
Values may be sent and summed in bfloat16 or wider, within the bound.
No kernel may reach another device: no remote copies, remote signals or barrier semaphores. Data moves between devices by JAX's collectives and lax.ppermute only.
A program may use at most 64 MiB of HBM per device.

```python
import math
import jax
import jax.numpy as jnp
from jax import lax

HD = 128
GROUP = 16
CACHE_DEV = 2048
NSPAN = 4
KVH = 8
TQ = 256
CACHE = 32768
N_CTX = 16


def draw_cache_k(key, part):
    key = jax.random.fold_in(key, 1)
    keys = jnp.clip(jax.random.normal(key, (KVH, CACHE_DEV * N_CTX, HD), jnp.float32), -4.0, 4.0)
    return keys.astype(jnp.bfloat16)


def draw_queries(key, part):
    key = jax.random.fold_in(key, 2)
    values = jnp.clip(3.0 * jax.random.normal(key, (TQ, KVH, GROUP, HD), jnp.float32), -12.0, 12.0)
    return values.astype(jnp.bfloat16)


def draw_span_bounds(key, part):
    key = jax.random.fold_in(key, 3)
    first_key, second_key = jax.random.split(key)
    region = TQ // NSPAN
    index = jnp.arange(NSPAN, dtype=jnp.int32)
    starts = index * region + jax.random.randint(first_key, (NSPAN,), 0, region // 4 + 1)
    widths = jax.random.randint(second_key, (NSPAN,), max(region // 4, 1), region // 2 + 1)
    return jnp.stack([starts, starts + widths], axis=1).astype(jnp.int32)


def draw_cache_len(key, part):
    key = jax.random.fold_in(key, 4)
    first_key, second_key = jax.random.split(key)
    lengths = jax.random.randint(first_key, (N_CTX,), CACHE_DEV // 4, CACHE_DEV + 1)
    full = jax.random.randint(second_key, (), 0, N_CTX)
    lengths = jnp.where(jnp.arange(N_CTX, dtype=jnp.int32) == full, CACHE_DEV, lengths)
    return lengths.astype(jnp.int32)


def shard_levels(key, extent, pieces, smallest, largest):
    def one(position, parts):
        heights = jax.random.uniform(jax.random.fold_in(jax.random.fold_in(key, 6), position), (parts,), jnp.float32, smallest / len(pieces), largest / len(pieces))
        return jnp.repeat(jnp.exp(heights), extent[position] // parts).reshape((-1,) + (1,) * (len(extent) - position - 1))

    loudness = one(*pieces[0])
    for cut in pieces[1:]:
        loudness = loudness * one(*cut)
    return loudness


def noise(stream_key, dims, width, limit, shards=(), held_as=jnp.bfloat16):
    array = width * jax.random.normal(stream_key, dims, jnp.float32)
    if shards:
        array = array * shard_levels(stream_key, dims, shards, -0.22, 0.18)
    return jnp.clip(array, -limit, limit).astype(held_as)


def setup_inputs(seed: int = 0, part: int = 0) -> dict:
    arg_keys = jax.random.split(jax.random.key(seed), 9)
    own_keys = jax.random.split(jax.random.fold_in(arg_keys[8], part), 9)
    queries = draw_queries(jax.random.fold_in(jax.random.fold_in(arg_keys[8], part), 71), part)
    new_keys = noise(own_keys[1], (TQ, KVH, HD), 1.4, 8.0, ((0, 16), (1, 8)))
    new_values = noise(own_keys[2], (TQ, KVH, HD), 1.0, 6.0, ((0, 16), (1, 8)))
    cache_k = draw_cache_k(jax.random.fold_in(jax.random.fold_in(arg_keys[8], part), 71), part)
    cache_v = noise(own_keys[4], (KVH, CACHE, HD), 1.0, 6.0, ((0, 8), (1, 16)))
    span_bounds = draw_span_bounds(jax.random.fold_in(jax.random.fold_in(arg_keys[8], part), 71), part)
    cache_len = draw_cache_len(jax.random.fold_in(jax.random.fold_in(arg_keys[8], part), 71), part)
    doc_start = jax.random.randint(own_keys[7], (1,), 0, CACHE_DEV * N_CTX // 8).astype(jnp.int32)
    return dict(queries=queries, new_keys=new_keys, new_values=new_values, cache_k=cache_k, cache_v=cache_v, span_bounds=span_bounds, cache_len=cache_len, doc_start=doc_start)


def reference(queries, new_keys, new_values, cache_k, cache_v, span_bounds, cache_len, doc_start):
    total_rows = CACHE_DEV * N_CTX
    rowids = jnp.arange(total_rows, dtype=jnp.int32)
    shard = rowids // CACHE_DEV
    slot = rowids % CACHE_DEV
    cache_ok = (slot < cache_len[shard]) & (slot * N_CTX + shard >= doc_start[0])
    tokens = jnp.arange(TQ, dtype=jnp.int32)
    inspan = (span_bounds[:, 0:1] <= tokens[None, :]) & (tokens[None, :] < span_bounds[:, 1:2])
    same_span = jnp.any(inspan[:, :, None] & inspan[:, None, :], axis=0)
    new_ok = (tokens[None, :] <= tokens[:, None]) | same_span
    scale = 1.0 / math.sqrt(HD)
    nblock = TQ // 16

    def one_block(index):
        head = index // nblock
        block = index % nblock
        first = (block * 16).astype(jnp.int32)
        head_q = lax.dynamic_index_in_dim(queries, head, axis=1, keepdims=False)
        qrows = lax.dynamic_slice_in_dim(head_q, first, 16, 0).reshape(16 * GROUP, HD)
        keys = lax.dynamic_index_in_dim(cache_k, head, axis=0, keepdims=False)
        values = lax.dynamic_index_in_dim(cache_v, head, axis=0, keepdims=False)
        fresh_k = lax.dynamic_index_in_dim(new_keys, head, axis=1, keepdims=False)
        fresh_v = lax.dynamic_index_in_dim(new_values, head, axis=1, keepdims=False)
        cache_sc = jnp.dot(qrows, keys.T, preferred_element_type=jnp.float32) * scale
        cache_sc = jnp.where(cache_ok[None, :], cache_sc, -1e+30)
        cache_sc = cache_sc.reshape(16 * GROUP, N_CTX, CACHE_DEV)
        shard_peak = lax.optimization_barrier(jnp.max(cache_sc, axis=2))
        cache_w = jnp.exp(cache_sc - shard_peak[:, :, None])
        shard_total = lax.optimization_barrier(jnp.sum(cache_w, axis=2))
        shard_lse = shard_peak + jnp.log(shard_total)
        weights16 = cache_w.astype(jnp.bfloat16).astype(jnp.float32)
        values_f = values.astype(jnp.float32).reshape(N_CTX, CACHE_DEV, HD)
        shard_numer = jnp.einsum('rsc,scd->rsd', weights16, values_f)
        shard_out = (shard_numer / shard_total[:, :, None]).astype(jnp.bfloat16).astype(jnp.float32)
        fresh_sc = jnp.dot(qrows, fresh_k.T, preferred_element_type=jnp.float32) * scale
        rows_ok = jnp.repeat(lax.dynamic_slice_in_dim(new_ok, first, 16, 0), GROUP, axis=0)
        fresh_sc = jnp.where(rows_ok, fresh_sc, -1e+30)
        fresh_peak = lax.optimization_barrier(jnp.max(fresh_sc, axis=1))
        fresh_w = jnp.exp(fresh_sc - fresh_peak[:, None])
        fresh_total = lax.optimization_barrier(jnp.sum(fresh_w, axis=1))
        fresh_numer = jnp.dot(fresh_w.astype(jnp.bfloat16), fresh_v, preferred_element_type=jnp.float32)
        top = jnp.maximum(fresh_peak, lax.optimization_barrier(jnp.max(shard_lse, axis=1)))
        factor = jnp.exp(shard_lse - top[:, None])
        fresh_f = jnp.exp(fresh_peak - top)
        totals = fresh_total * fresh_f + lax.optimization_barrier(jnp.sum(factor, axis=1))
        numer = fresh_numer * fresh_f[:, None] + lax.optimization_barrier(jnp.sum(shard_out * factor[:, :, None], axis=1))
        return (numer / totals[:, None]).astype(jnp.bfloat16).reshape(16, GROUP, HD)
    result = lax.map(one_block, jnp.arange(KVH * nblock, dtype=jnp.int32))
    result = result.reshape(KVH, nblock, 16, GROUP, HD).transpose(1, 2, 0, 3, 4)
    return result.reshape(TQ, KVH, GROUP, HD)
```

```python
import functools
import math

import jax
import jax.numpy as jnp
from jax import lax
from jax.experimental import pallas as pl
from jax.experimental.pallas import tpu as pltpu
from jax.sharding import Mesh
from jax.sharding import PartitionSpec as P

F32 = jnp.float32
BF16 = jnp.bfloat16
HIDDEN = -1e30
CHUNK = 1024
TILE = 128
EXTRA = 16
NT = (((1,), (1,)), ((), ()))


def pieces(x):
    hi = x.astype(BF16).astype(F32)
    mid = (x - hi).astype(BF16).astype(F32)
    return hi, mid, x - hi - mid


def write_message(out, numer, peak, total):
    dim = numer.shape[0]
    out[0:dim, :] = numer.astype(BF16)
    row = lax.broadcasted_iota(jnp.int32, (EXTRA, numer.shape[1]), 0)
    tail = jnp.zeros((EXTRA, numer.shape[1]), F32)
    for at, piece in enumerate(pieces(peak) + pieces(total)):
        tail = jnp.where(row == at, piece, tail)
    out[dim : dim + EXTRA, :] = tail.astype(BF16)


def read_message(ref):
    dim = ref.shape[0] - EXTRA
    tail = ref[dim : dim + EXTRA, :].astype(F32)
    peak = tail[0:1] + tail[1:2] + tail[2:3]
    total = tail[3:4] + tail[4:5] + tail[5:6]
    return ref[0:dim, :].astype(F32), peak, total


def merge(refs):
    parts = [read_message(ref) for ref in refs]
    peak = functools.reduce(jnp.maximum, [p[1] for p in parts])
    factors = [jnp.exp2(p[1] - peak) for p in parts]
    total = sum(p[2] * f for p, f in zip(parts, factors))
    numer = sum(p[0] * f for p, f in zip(parts, factors))
    return numer, peak, total


def pack_kernel(count, where, *refs):
    k_hbm, v_hbm, nk_hbm, nv_hbm, q_hbm, cache_len, doc_start = refs[:7]
    pack, rep = refs[7:9]
    kbuf, vbuf, nvbuf, qsem, ksem, vsem, nsem = refs[9:]
    rows, dim = kbuf.shape
    new = nvbuf.shape[0]
    me = where()
    first = lax.div(jnp.maximum(doc_start[0] - me + count - 1, 0), count)
    limit = cache_len[me]

    q_copies = [pltpu.make_async_copy(q_hbm, rep.at[j], qsem.at[j]) for j in range(rep.shape[0])]
    k_copy = pltpu.make_async_copy(k_hbm.at[0], kbuf, ksem)
    v_copy = pltpu.make_async_copy(v_hbm.at[0], vbuf, vsem)
    nk_copy = pltpu.make_async_copy(nk_hbm, pack.at[pl.ds(rows, new)], nsem.at[0])
    nv_copy = pltpu.make_async_copy(nv_hbm, nvbuf, nsem.at[1])
    copies = [*q_copies, nk_copy, nv_copy]
    for copy in [k_copy, v_copy, *copies]:
        copy.start()

    safe = rows // 8
    step = 4 * TILE
    base = rows + new
    k_copy.wait()
    spare = kbuf[safe : safe + 16, :][0:1].astype(F32)
    for at in range(0, rows, step):
        slot = lax.broadcasted_iota(jnp.int32, (step, dim), 0) + at
        ok = (slot >= first) & (slot < limit)
        pack[at : at + step, :] = jnp.where(ok, kbuf[at : at + step, :].astype(F32), spare).astype(BF16)
    v_copy.wait()
    for at in range(0, rows, TILE):
        to = base + at // TILE * (dim + EXTRA)
        slot = lax.broadcasted_iota(jnp.int32, (TILE, dim), 0) + at
        ok = (slot >= first) & (slot < limit)
        values = jnp.where(ok, vbuf[at : at + TILE, :].astype(F32), 0.0)
        pack[to : to + dim, :] = values.T.astype(BF16)
        slot = lax.broadcasted_iota(jnp.int32, (EXTRA, TILE), 1) + at
        row = lax.broadcasted_iota(jnp.int32, (EXTRA, TILE), 0)
        ok = (slot >= first) & (slot < limit) & (row == 0)
        pack[to + dim : to + dim + EXTRA, :] = jnp.where(ok, 1.0, 0.0).astype(BF16)
    for copy in copies:
        copy.wait()
    to = base + rows // TILE * (dim + EXTRA)
    odd = lax.rem(me, 2) == 1
    own = nvbuf[...].astype(F32)
    none = jnp.zeros_like(own)
    both = [jnp.where(odd, none, own), jnp.where(odd, own, none), jnp.zeros((TILE - 2 * new, dim), F32)]
    pack[to : to + dim, :] = jnp.concatenate(both, axis=0).T.astype(BF16)
    row = lax.broadcasted_iota(jnp.int32, (EXTRA, TILE), 0)
    column = lax.broadcasted_iota(jnp.int32, (EXTRA, TILE), 1)
    mine = lax.div(column, new) == lax.rem(me, 2)
    pack[to + dim : to + dim + EXTRA, :] = jnp.where((row == 0) & mine, 1.0, 0.0).astype(BF16)


def fresh_mask(me, owner, spans, new, group, rows):
    key = lax.broadcasted_iota(jnp.int32, (2 * new, rows), 0) + (me - lax.rem(me, 2)) * new
    token = lax.div(lax.broadcasted_iota(jnp.int32, (1, rows), 1), group) + owner * new
    ok = key <= token
    for k in range(spans.shape[1]):
        lo, hi = spans[0, k], spans[1, k]
        ok = ok | ((token >= lo) & (token < hi) & (key >= lo) & (key < hi))
    return ok


def attend_kernel(where, away, cache_dev, new, group, scale2, spans, own, other, q_ref, out, s0, s1, fresh_k, fresh_v):
    n, rows, dim = q_ref.shape
    me = where()
    core = lax.rem(me, 2)
    quad = (me - lax.rem(me, 2 * n)) ^ (2 * n if away else 0)
    base = cache_dev + new
    tall = dim + EXTRA
    s_refs = (s0, s1)

    odd = core == 1
    mine, theirs = own[cache_dev:base, :].astype(F32), other[cache_dev:base, :].astype(F32)
    fresh_k[0:new, :] = jnp.where(odd, theirs, mine).astype(BF16)
    fresh_k[new : 2 * new, :] = jnp.where(odd, mine, theirs).astype(BF16)
    at = base + cache_dev // TILE * tall
    fresh_v[...] = (own[at : at + tall, :].astype(F32) + other[at : at + tall, :].astype(F32)).astype(BF16)

    tiles = [(which, at) for which in (0, 1) for at in range(0, cache_dev, CHUNK)] + [None]

    def scores(b, tile, peak):
        if tile is None:
            s = lax.dot_general(fresh_k[...], q_ref[b], NT, preferred_element_type=F32)
            s = jnp.where(fresh_mask(me, quad + 2 * b + core, spans, new, group, rows), s, HIDDEN)
            to, size = 2 * cache_dev, 2 * new
        else:
            which, at = tile
            s = lax.dot_general((own, other)[which][at : at + CHUNK, :], q_ref[b], NT, preferred_element_type=F32)
            to, size = which * cache_dev + at, CHUNK
        s_refs[b % 2][to : to + size, :] = s
        top = jnp.max(s.reshape(size // 8, 8, rows), axis=0)
        return top if peak is None else jnp.maximum(peak, top)

    def weigh(b, tile, peak, acc):
        if tile is None:
            s = s_refs[b % 2][2 * cache_dev : 2 * cache_dev + 2 * new, :]
            p = jnp.exp2((s - peak) * scale2)
            p = jnp.concatenate([p, jnp.zeros((TILE - 2 * new, rows), F32)], axis=0).astype(BF16)
            v = fresh_v[...]
        else:
            which, at = tile
            to = which * cache_dev + at
            p = jnp.exp2((s_refs[b % 2][to : to + CHUNK, :] - peak) * scale2).astype(BF16)
            starts = [base + (at // TILE + j) * tall for j in range(CHUNK // TILE)]
            v = jnp.concatenate([(own, other)[which][i : i + tall, :] for i in starts], axis=1)
        o = jnp.dot(v, p, preferred_element_type=F32)
        return o if acc is None else acc + o

    peak = None
    for tile in tiles:
        peak = scores(0, tile, peak)
    for b in range(n):
        top = jnp.max(peak, axis=0, keepdims=True)
        acc, peak = None, None
        for tile in tiles:
            acc = weigh(b, tile, top, acc)
            if b + 1 < n:
                peak = scores(b + 1, tile, peak)
        write_message(out.at[b], acc[0:dim], top * scale2, acc[dim : dim + 1])


def merge_kernel(got, out):
    write_message(out, *merge([got.at[j] for j in range(got.shape[0])]))


def final_kernel(got, back, out):
    numer, _, total = merge([got.at[j] for j in range(got.shape[0])] + [back])
    out[...] = (numer / total).T.astype(BF16)


def on_device(queries, new_keys, new_values, cache_k, cache_v, span_bounds, cache_len, doc_start):
    far, near, cores = (lax.axis_size(name) for name in ("far", "near", "core"))
    new, _, group, dim = queries.shape
    rows = new * group
    cache_dev = cache_k.shape[1]
    packed = cache_dev + new + (cache_dev // TILE + 1) * (dim + EXTRA)
    scale2 = math.log2(math.e) / math.sqrt(dim)

    def where():
        return (lax.axis_index("far") * near + lax.axis_index("near")) * cores + lax.axis_index("core")

    def across(x, axis):
        return lax.ppermute(x, axis, [(0, 1), (1, 0)])

    def quad(x):
        return lax.all_to_all(x, "near", split_axis=0, concat_axis=0, tiled=True)

    hbm = pl.BlockSpec(memory_space=pltpu.HBM)
    vmem = pl.BlockSpec(memory_space=pltpu.VMEM)
    smem = pl.BlockSpec(memory_space=pltpu.SMEM)
    params = pltpu.CompilerParams(vmem_limit_bytes=32 * 1024 * 1024)
    message = jax.ShapeDtypeStruct((dim + EXTRA, rows), BF16)
    dma = pltpu.SemaphoreType.DMA

    q = queries.reshape(rows, dim)
    q_far = across(q, "far")
    own, q_rep = pl.pallas_call(
        functools.partial(pack_kernel, far * near * cores, where),
        out_shape=[jax.ShapeDtypeStruct((packed, dim), BF16), jax.ShapeDtypeStruct((near, rows, dim), BF16)],
        in_specs=[hbm] * 5 + [smem] * 2,
        out_specs=[vmem] * 2,
        scratch_shapes=[
            pltpu.VMEM((cache_dev, dim), BF16),
            pltpu.VMEM((cache_dev, dim), BF16),
            pltpu.VMEM((new, dim), BF16),
            dma((near,)),
            dma,
            dma,
            dma((2,)),
        ],
        compiler_params=params,
        name="pack",
    )(cache_k, cache_v, new_keys.reshape(new, dim), new_values.reshape(new, dim), q, cache_len, doc_start)
    q_near = quad(q_rep)
    other = across(own, "core")
    q_far = quad(jnp.broadcast_to(q_far[None], (near, rows, dim)))

    spans = span_bounds.T
    cost = pl.CostEstimate(
        flops=4 * near * rows * 2 * cache_dev * dim,
        bytes_accessed=4 << 20,
        transcendentals=near * rows * 2 * cache_dev,
    )

    def attend(blocks, away, name):
        return pl.pallas_call(
            functools.partial(attend_kernel, where, away, cache_dev, new, group, scale2),
            out_shape=jax.ShapeDtypeStruct((near,) + message.shape, BF16),
            in_specs=[smem] + [vmem] * 3,
            out_specs=vmem,
            scratch_shapes=[pltpu.VMEM((2 * cache_dev + 2 * new, rows), F32)] * 2
            + [pltpu.VMEM((2 * new, dim), BF16), pltpu.VMEM((dim + EXTRA, TILE), BF16)],
            compiler_params=params,
            cost_estimate=cost,
            name=name,
        )(spans, own, other, blocks)

    near_out = attend(q_near, False, "near_blocks")
    far_out = attend(q_far, True, "far_blocks")
    far_got = quad(far_out)
    near_got = quad(near_out)
    far_sum = pl.pallas_call(
        merge_kernel, out_shape=message, in_specs=[vmem], out_specs=vmem, compiler_params=params, name="merge_far"
    )(far_got)
    back = across(far_sum, "far")
    result = pl.pallas_call(
        final_kernel,
        out_shape=jax.ShapeDtypeStruct((rows, dim), BF16),
        in_specs=[vmem] * 2,
        out_specs=vmem,
        compiler_params=params,
        name="merge_all",
    )(near_got, back)
    return result.reshape(new, 1, group, dim)


def solution(mesh):
    ctx, kvh, sess = (mesh.shape[name] for name in ("ctx", "kvh", "sess"))
    devices = mesh.devices.reshape(2, ctx // 4, 2, kvh, sess)
    split = Mesh(devices, ("far", "near", "core", "kvh", "sess"))
    ctx = ("far", "near", "core")
    return jax.shard_map(
        on_device,
        mesh=split,
        in_specs=(
            P(("sess",) + ctx, "kvh", None, None),
            P(("sess",) + ctx, "kvh", None),
            P(("sess",) + ctx, "kvh", None),
            P(("sess", "kvh"), ctx, None),
            P(("sess", "kvh"), ctx, None),
            P("sess", None),
            P("sess"),
            P("sess"),
        ),
        out_specs=P(("sess",) + ctx, "kvh", None, None),
        check_vma=False,
    )
```

```python
import functools
import math

import jax
import jax.numpy as jnp
from jax import lax
from jax.experimental import pallas as pl
from jax.experimental.pallas import tpu as pltpu
from jax.sharding import Mesh
from jax.sharding import PartitionSpec as P

F32 = jnp.float32
BF16 = jnp.bfloat16
HIDDEN = -1e30
CHUNK = 512
TILE = 128
WIDE = 512
EXTRA = 16
NT = (((1,), (1,)), ((), ()))


def pieces(x):
    hi = x.astype(BF16).astype(F32)
    mid = (x - hi).astype(BF16).astype(F32)
    return hi, mid, x - hi - mid


def write_message(out, numer, peak, total):
    dim = numer.shape[0]
    out[0:dim, :] = numer.astype(BF16)
    row = lax.broadcasted_iota(jnp.int32, (EXTRA, numer.shape[1]), 0)
    tail = jnp.zeros((EXTRA, numer.shape[1]), F32)
    for at, piece in enumerate(pieces(peak) + pieces(total)):
        tail = jnp.where(row == at, piece, tail)
    out[dim : dim + EXTRA, :] = tail.astype(BF16)


def read_message(ref):
    dim = ref.shape[0] - EXTRA
    tail = ref[dim : dim + EXTRA, :].astype(F32)
    peak = tail[0:1] + tail[1:2] + tail[2:3]
    total = tail[3:4] + tail[4:5] + tail[5:6]
    return ref[0:dim, :].astype(F32), peak, total


def merge(refs):
    parts = [read_message(ref) for ref in refs]
    peak = functools.reduce(jnp.maximum, [p[1] for p in parts])
    factors = [jnp.exp2(p[1] - peak) for p in parts]
    total = sum(p[2] * f for p, f in zip(parts, factors))
    numer = sum(p[0] * f for p, f in zip(parts, factors))
    return numer, peak, total


def pack_kernel(count, where, *refs):
    k_hbm, v_hbm, nk_hbm, nv_hbm, cache_len, doc_start, pack = refs[:7]
    kbuf, vbuf, nvbuf, ksem, vsem, nsem = refs[7:]
    rows, dim = kbuf.shape
    new = nvbuf.shape[0]
    me = where()
    first = lax.div(jnp.maximum(doc_start[0] - me + count - 1, 0), count)
    limit = cache_len[me]

    k_copy = pltpu.make_async_copy(k_hbm.at[0], kbuf, ksem)
    v_copy = pltpu.make_async_copy(v_hbm.at[0], vbuf, vsem)
    nk_copy = pltpu.make_async_copy(nk_hbm, pack.at[pl.ds(rows, new)], nsem.at[0])
    nv_copy = pltpu.make_async_copy(nv_hbm, nvbuf, nsem.at[1])
    copies = [nk_copy, nv_copy]
    for copy in [k_copy, v_copy, *copies]:
        copy.start()

    safe = rows // 8
    step = 4 * TILE
    base = rows + new
    k_copy.wait()
    spare = kbuf[safe : safe + 16, :][0:1].astype(F32)
    for at in range(0, rows, step):
        slot = lax.broadcasted_iota(jnp.int32, (step, dim), 0) + at
        ok = (slot >= first) & (slot < limit)
        pack[at : at + step, :] = jnp.where(ok, kbuf[at : at + step, :].astype(F32), spare).astype(BF16)
    v_copy.wait()
    for at in range(0, rows, TILE):
        to = base + at // TILE * (dim + EXTRA)
        slot = lax.broadcasted_iota(jnp.int32, (TILE, dim), 0) + at
        ok = (slot >= first) & (slot < limit)
        values = jnp.where(ok, vbuf[at : at + TILE, :].astype(F32), 0.0)
        pack[to : to + dim, :] = values.T.astype(BF16)
        slot = lax.broadcasted_iota(jnp.int32, (EXTRA, TILE), 1) + at
        row = lax.broadcasted_iota(jnp.int32, (EXTRA, TILE), 0)
        ok = (slot >= first) & (slot < limit) & (row == 0)
        pack[to + dim : to + dim + EXTRA, :] = jnp.where(ok, 1.0, 0.0).astype(BF16)
    for copy in copies:
        copy.wait()
    to = base + rows // TILE * (dim + EXTRA)
    odd = lax.rem(me, 2) == 1
    own = nvbuf[...].astype(F32)
    none = jnp.zeros_like(own)
    both = [jnp.where(odd, none, own), jnp.where(odd, own, none), jnp.zeros((TILE - 2 * new, dim), F32)]
    pack[to : to + dim, :] = jnp.concatenate(both, axis=0).T.astype(BF16)
    row = lax.broadcasted_iota(jnp.int32, (EXTRA, TILE), 0)
    column = lax.broadcasted_iota(jnp.int32, (EXTRA, TILE), 1)
    mine = lax.div(column, new) == lax.rem(me, 2)
    pack[to + dim : to + dim + EXTRA, :] = jnp.where((row == 0) & mine, 1.0, 0.0).astype(BF16)


def fresh_mask(me, token, spans, new):
    key = lax.broadcasted_iota(jnp.int32, (2 * new, token.shape[1]), 0) + (me - lax.rem(me, 2)) * new
    ok = key <= token
    for k in range(spans.shape[1]):
        lo, hi = spans[0, k], spans[1, k]
        ok = ok | ((token >= lo) & (token < hi) & (key >= lo) & (key < hi))
    return ok


def attend_kernel(where, away, cache_dev, new, group, scale2, spans, own, other, q_ref, out, s0, s1, fresh_k, fresh_v):
    members, part, dim = q_ref.shape
    pair = WIDE // part
    n, rows = members // pair, WIDE
    me = where()
    core = lax.rem(me, 2)
    quad = (me - lax.rem(me, 2 * members)) ^ (2 * members if away else 0)
    base = cache_dev + new
    tall = dim + EXTRA
    s_refs = (s0, s1)

    odd = core == 1
    mine, theirs = own[cache_dev:base, :].astype(F32), other[cache_dev:base, :].astype(F32)
    fresh_k[0:new, :] = jnp.where(odd, theirs, mine).astype(BF16)
    fresh_k[new : 2 * new, :] = jnp.where(odd, mine, theirs).astype(BF16)
    at = base + cache_dev // TILE * tall
    fresh_v[...] = (own[at : at + tall, :].astype(F32) + other[at : at + tall, :].astype(F32)).astype(BF16)

    tiles = [(which, at) for which in (0, 1) for at in range(0, cache_dev, CHUNK)] + [None]

    def block(b):
        return q_ref[pair * b : pair * (b + 1)].reshape(rows, dim)

    def scores(b, tile, peak):
        if tile is None:
            s = lax.dot_general(fresh_k[...], block(b), NT, preferred_element_type=F32)
            lane = lax.broadcasted_iota(jnp.int32, (1, rows), 1)
            owner = quad + (pair * b + lax.div(lane, part)) * 2 + core
            token = owner * new + lax.div(lax.rem(lane, part), group)
            s = jnp.where(fresh_mask(me, token, spans, new), s, HIDDEN)
            to, size = 2 * cache_dev, 2 * new
        else:
            which, at = tile
            s = lax.dot_general((own, other)[which][at : at + CHUNK, :], block(b), NT, preferred_element_type=F32)
            to, size = which * cache_dev + at, CHUNK
        s_refs[b % 2][to : to + size, :] = s
        top = jnp.max(s.reshape(size // 8, 8, rows), axis=0)
        return top if peak is None else jnp.maximum(peak, top)

    def weigh(b, tile, peak, acc):
        if tile is None:
            s = s_refs[b % 2][2 * cache_dev : 2 * cache_dev + 2 * new, :]
            p = jnp.exp2((s - peak) * scale2)
            p = jnp.concatenate([p, jnp.zeros((TILE - 2 * new, rows), F32)], axis=0).astype(BF16)
            v = fresh_v[...]
        else:
            which, at = tile
            to = which * cache_dev + at
            p = jnp.exp2((s_refs[b % 2][to : to + CHUNK, :] - peak) * scale2).astype(BF16)
            starts = [base + (at // TILE + j) * tall for j in range(CHUNK // TILE)]
            v = jnp.concatenate([(own, other)[which][i : i + tall, :] for i in starts], axis=1)
        o = jnp.dot(v, p, preferred_element_type=F32)
        return o if acc is None else acc + o

    peak = None
    for tile in tiles:
        peak = scores(0, tile, peak)
    for b in range(n):
        top = jnp.max(peak, axis=0, keepdims=True)
        acc, peak = None, None
        for tile in tiles:
            acc = weigh(b, tile, top, acc)
            if b + 1 < n:
                peak = scores(b + 1, tile, peak)
        for j in range(pair):
            cut = slice(j * part, (j + 1) * part)
            write_message(out.at[pair * b + j], acc[0:dim, cut], top[:, cut] * scale2, acc[dim : dim + 1, cut])


def spread_kernel(q, q_far, _, near_out, far_out):
    for j in range(near_out.shape[0]):
        near_out[j] = q[...]
        far_out[j] = q_far[...]


def merge_kernel(got, _, out, kept):
    write_message(out, *merge([got.at[j] for j in range(got.shape[0])]))


def final_kernel(got, back, out):
    numer, _, total = merge([got.at[j] for j in range(got.shape[0])] + [back])
    out[...] = (numer / total).T.astype(BF16)


def on_device(queries, new_keys, new_values, cache_k, cache_v, span_bounds, cache_len, doc_start):
    far, near, cores = (lax.axis_size(name) for name in ("far", "near", "core"))
    new, _, group, dim = queries.shape
    rows = new * group
    cache_dev = cache_k.shape[1]
    packed = cache_dev + new + (cache_dev // TILE + 1) * (dim + EXTRA)
    scale2 = math.log2(math.e) / math.sqrt(dim)

    def where():
        return (lax.axis_index("far") * near + lax.axis_index("near")) * cores + lax.axis_index("core")

    def across(x, axis):
        return lax.ppermute(x, axis, [(0, 1), (1, 0)])

    def quad(x):
        return lax.all_to_all(x, "near", split_axis=0, concat_axis=0, tiled=True)

    hbm = pl.BlockSpec(memory_space=pltpu.HBM)
    vmem = pl.BlockSpec(memory_space=pltpu.VMEM)
    smem = pl.BlockSpec(memory_space=pltpu.SMEM)
    params = pltpu.CompilerParams(vmem_limit_bytes=40 * 1024 * 1024)
    message = jax.ShapeDtypeStruct((dim + EXTRA, rows), BF16)
    dma = pltpu.SemaphoreType.DMA

    q = queries.reshape(rows, dim)
    q_far = across(q, "far")
    own = pl.pallas_call(
        functools.partial(pack_kernel, far * near * cores, where),
        out_shape=jax.ShapeDtypeStruct((packed, dim), BF16),
        in_specs=[hbm] * 4 + [smem] * 2,
        out_specs=vmem,
        scratch_shapes=[
            pltpu.VMEM((cache_dev, dim), BF16),
            pltpu.VMEM((cache_dev, dim), BF16),
            pltpu.VMEM((new, dim), BF16),
            dma,
            dma,
            dma((2,)),
        ],
        compiler_params=params,
        name="pack",
    )(cache_k, cache_v, new_keys.reshape(new, dim), new_values.reshape(new, dim), cache_len, doc_start)
    slots = jax.ShapeDtypeStruct((near, rows, dim), BF16)
    q_near, q_far = pl.pallas_call(
        spread_kernel,
        out_shape=[slots] * 2,
        in_specs=[vmem, vmem, pl.BlockSpec(memory_space=pl.ANY)],
        out_specs=[vmem] * 2,
        compiler_params=params,
        name="spread",
    )(q, q_far, own)
    q_far = quad(q_far)
    other = across(own, "core")
    q_near = quad(q_near)

    spans = span_bounds.T
    cost = pl.CostEstimate(
        flops=4 * near * rows * 2 * cache_dev * dim,
        bytes_accessed=4 << 20,
        transcendentals=near * rows * 2 * cache_dev,
    )

    def attend(blocks, away, name):
        return pl.pallas_call(
            functools.partial(attend_kernel, where, away, cache_dev, new, group, scale2),
            out_shape=jax.ShapeDtypeStruct((near,) + message.shape, BF16),
            in_specs=[smem] + [vmem] * 3,
            out_specs=vmem,
            scratch_shapes=[pltpu.VMEM((2 * cache_dev + 2 * new, WIDE), F32)] * 2
            + [pltpu.VMEM((2 * new, dim), BF16), pltpu.VMEM((dim + EXTRA, TILE), BF16)],
            compiler_params=params,
            cost_estimate=cost,
            name=name,
        )(spans, own, other, blocks)

    far_out = attend(q_far, True, "far_blocks")
    far_got = quad(far_out)
    near_out = attend(q_near, False, "near_blocks")
    anywhere = pl.BlockSpec(memory_space=pl.ANY)
    far_sum, near_out = pl.pallas_call(
        merge_kernel,
        out_shape=[message, jax.ShapeDtypeStruct(near_out.shape, BF16)],
        in_specs=[vmem, anywhere],
        out_specs=[vmem, anywhere],
        input_output_aliases={1: 1},
        compiler_params=params,
        name="merge_far",
    )(far_got, near_out)
    back = across(far_sum, "far")
    near_got = quad(near_out)
    result = pl.pallas_call(
        final_kernel,
        out_shape=jax.ShapeDtypeStruct((rows, dim), BF16),
        in_specs=[vmem] * 2,
        out_specs=vmem,
        compiler_params=params,
        name="merge_all",
    )(near_got, back)
    return result.reshape(new, 1, group, dim)


def solution(mesh):
    ctx, kvh, sess = (mesh.shape[name] for name in ("ctx", "kvh", "sess"))
    devices = mesh.devices.reshape(2, ctx // 4, 2, kvh, sess)
    split = Mesh(devices, ("far", "near", "core", "kvh", "sess"))
    ctx = ("far", "near", "core")
    return jax.shard_map(
        on_device,
        mesh=split,
        in_specs=(
            P(("sess",) + ctx, "kvh", None, None),
            P(("sess",) + ctx, "kvh", None),
            P(("sess",) + ctx, "kvh", None),
            P(("sess", "kvh"), ctx, None),
            P(("sess", "kvh"), ctx, None),
            P("sess", None),
            P("sess"),
            P("sess"),
        ),
        out_specs=P(("sess",) + ctx, "kvh", None, None),
        check_vma=False,
    )
```

```python
import functools
import math

import jax
import jax.numpy as jnp
from jax import lax
from jax.experimental import pallas as pl
from jax.experimental.pallas import tpu as pltpu
from jax.sharding import Mesh
from jax.sharding import PartitionSpec as P

F32 = jnp.float32
BF16 = jnp.bfloat16
HIDDEN = -1e30
CHUNK = 256
TILE = 128
WIDE = 512
EXTRA = 16
NT = (((1,), (1,)), ((), ()))


def pieces(x):
    hi = x.astype(BF16).astype(F32)
    mid = (x - hi).astype(BF16).astype(F32)
    return hi, mid, x - hi - mid


def write_message(out, numer, peak, total):
    dim = numer.shape[0]
    out[0:dim, :] = numer.astype(BF16)
    row = lax.broadcasted_iota(jnp.int32, (EXTRA, numer.shape[1]), 0)
    tail = jnp.zeros((EXTRA, numer.shape[1]), F32)
    for at, piece in enumerate(pieces(peak) + pieces(total)):
        tail = jnp.where(row == at, piece, tail)
    out[dim : dim + EXTRA, :] = tail.astype(BF16)


def read_message(ref):
    dim = ref.shape[0] - EXTRA
    tail = ref[dim : dim + EXTRA, :].astype(F32)
    peak = tail[0:1] + tail[1:2] + tail[2:3]
    total = tail[3:4] + tail[4:5] + tail[5:6]
    return ref[0:dim, :].astype(F32), peak, total


def merge(refs):
    parts = [read_message(ref) for ref in refs]
    peak = functools.reduce(jnp.maximum, [p[1] for p in parts])
    factors = [jnp.exp2(p[1] - peak) for p in parts]
    total = sum(p[2] * f for p, f in zip(parts, factors))
    numer = sum(p[0] * f for p, f in zip(parts, factors))
    return numer, peak, total


def pack_kernel(count, where, *refs):
    k_hbm, v_hbm, nk_hbm, nv_hbm, cache_len, doc_start, pack = refs[:7]
    kbuf, vbuf, nvbuf, ksem, vsem, nsem = refs[7:]
    rows, dim = kbuf.shape
    new = nvbuf.shape[0]
    me = where()
    first = lax.div(jnp.maximum(doc_start[0] - me + count - 1, 0), count)
    limit = cache_len[me]

    k_copy = pltpu.make_async_copy(k_hbm.at[0], kbuf, ksem)
    v_copy = pltpu.make_async_copy(v_hbm.at[0], vbuf, vsem)
    nk_copy = pltpu.make_async_copy(nk_hbm, pack.at[pl.ds(rows, new)], nsem.at[0])
    nv_copy = pltpu.make_async_copy(nv_hbm, nvbuf, nsem.at[1])
    copies = [nk_copy, nv_copy]
    for copy in [k_copy, v_copy, *copies]:
        copy.start()

    safe = rows // 8
    step = 4 * TILE
    base = rows + new
    k_copy.wait()
    spare = kbuf[safe : safe + 16, :][0:1].astype(F32)
    for at in range(0, rows, step):
        slot = lax.broadcasted_iota(jnp.int32, (step, dim), 0) + at
        ok = (slot >= first) & (slot < limit)
        pack[at : at + step, :] = jnp.where(ok, kbuf[at : at + step, :].astype(F32), spare).astype(BF16)
    v_copy.wait()
    for at in range(0, rows, TILE):
        to = base + at // TILE * (dim + EXTRA)
        slot = lax.broadcasted_iota(jnp.int32, (TILE, dim), 0) + at
        ok = (slot >= first) & (slot < limit)
        values = jnp.where(ok, vbuf[at : at + TILE, :].astype(F32), 0.0)
        pack[to : to + dim, :] = values.T.astype(BF16)
        slot = lax.broadcasted_iota(jnp.int32, (EXTRA, TILE), 1) + at
        row = lax.broadcasted_iota(jnp.int32, (EXTRA, TILE), 0)
        ok = (slot >= first) & (slot < limit) & (row == 0)
        pack[to + dim : to + dim + EXTRA, :] = jnp.where(ok, 1.0, 0.0).astype(BF16)
    for copy in copies:
        copy.wait()
    to = base + rows // TILE * (dim + EXTRA)
    odd = lax.rem(me, 2) == 1
    own = nvbuf[...].astype(F32)
    none = jnp.zeros_like(own)
    both = [jnp.where(odd, none, own), jnp.where(odd, own, none), jnp.zeros((TILE - 2 * new, dim), F32)]
    pack[to : to + dim, :] = jnp.concatenate(both, axis=0).T.astype(BF16)
    row = lax.broadcasted_iota(jnp.int32, (EXTRA, TILE), 0)
    column = lax.broadcasted_iota(jnp.int32, (EXTRA, TILE), 1)
    mine = lax.div(column, new) == lax.rem(me, 2)
    pack[to + dim : to + dim + EXTRA, :] = jnp.where((row == 0) & mine, 1.0, 0.0).astype(BF16)


def fresh_mask(me, token, spans, new):
    key = lax.broadcasted_iota(jnp.int32, (2 * new, token.shape[1]), 0) + (me - lax.rem(me, 2)) * new
    ok = key <= token
    for k in range(spans.shape[1]):
        lo, hi = spans[0, k], spans[1, k]
        ok = ok | ((token >= lo) & (token < hi) & (key >= lo) & (key < hi))
    return ok


def attend_kernel(where, away, cache_dev, new, group, scale2, spans, own, other, q_ref, out, s0, s1, acc, fresh_k, fresh_v):
    members, part, dim = q_ref.shape
    pair = WIDE // part
    n, rows = members // pair, WIDE
    me = where()
    core = lax.rem(me, 2)
    quad = (me - lax.rem(me, 2 * members)) ^ (2 * members if away else 0)
    base = cache_dev + new
    tall = dim + EXTRA
    s_refs = (s0, s1)
    halves = (own, other)

    odd = core == 1
    mine, theirs = own[cache_dev:base, :].astype(F32), other[cache_dev:base, :].astype(F32)
    fresh_k[0:new, :] = jnp.where(odd, theirs, mine).astype(BF16)
    fresh_k[new : 2 * new, :] = jnp.where(odd, mine, theirs).astype(BF16)
    at = base + cache_dev // TILE * tall
    fresh_v[...] = (own[at : at + tall, :].astype(F32) + other[at : at + tall, :].astype(F32)).astype(BF16)

    def block(b):
        return q_ref[pair * b : pair * (b + 1)].reshape(rows, dim)

    def top_of(s):
        return jnp.max(s.reshape(s.shape[0] // 8, 8, rows), axis=0)

    def fresh_scores(b):
        s = lax.dot_general(fresh_k[...], block(b), NT, preferred_element_type=F32)
        lane = lax.broadcasted_iota(jnp.int32, (1, rows), 1)
        owner = quad + (pair * b + lax.div(lane, part)) * 2 + core
        token = owner * new + lax.div(lax.rem(lane, part), group)
        s = jnp.where(fresh_mask(me, token, spans, new), s, HIDDEN)
        s_refs[b % 2][2 * cache_dev : 2 * cache_dev + 2 * new, :] = s
        return top_of(s)

    def scores(b, i, peak):
        for which, ref in enumerate(halves):
            keys = ref[pl.ds(pl.multiple_of(i * CHUNK, CHUNK), CHUNK), :]
            s = lax.dot_general(keys, block(b), NT, preferred_element_type=F32)
            s_refs[b % 2][pl.ds(pl.multiple_of(which * cache_dev + i * CHUNK, CHUNK), CHUNK), :] = s
            peak = jnp.maximum(peak, top_of(s))
        return peak

    def fresh_weigh(b, peak):
        s = s_refs[b % 2][2 * cache_dev : 2 * cache_dev + 2 * new, :]
        p = jnp.exp2((s - peak) * scale2)
        p = jnp.concatenate([p, jnp.zeros((TILE - 2 * new, rows), F32)], axis=0).astype(BF16)
        acc[...] = jnp.dot(fresh_v[...], p, preferred_element_type=F32)

    def weigh(b, i, peak):
        ps, vs = [], []
        for which, ref in enumerate(halves):
            s = s_refs[b % 2][pl.ds(pl.multiple_of(which * cache_dev + i * CHUNK, CHUNK), CHUNK), :]
            ps.append(jnp.exp2((s - peak) * scale2).astype(BF16))
            for j in range(CHUNK // TILE):
                vs.append(ref[pl.ds(pl.multiple_of(base + (i * (CHUNK // TILE) + j) * tall, 16), tall), :])
        acc[...] += jnp.dot(jnp.concatenate(vs, axis=1), jnp.concatenate(ps, axis=0), preferred_element_type=F32)

    steps = cache_dev // CHUNK
    peak = lax.fori_loop(0, steps, lambda i, peak: scores(0, i, peak), fresh_scores(0))
    for b in range(n):
        top = jnp.max(peak, axis=0, keepdims=True)
        fresh_weigh(b, top)
        if b + 1 < n:

            def both(i, peak, b=b, top=top):
                weigh(b, i, top)
                return scores(b + 1, i, peak)

            peak = lax.fori_loop(0, steps, both, fresh_scores(b + 1))
        else:

            def last(i, carry, b=b, top=top):
                weigh(b, i, top)
                return carry

            lax.fori_loop(0, steps, last, 0)
        for j in range(pair):
            cut = slice(j * part, (j + 1) * part)
            write_message(out.at[pair * b + j], acc[0:dim, cut], top[:, cut] * scale2, acc[dim : dim + 1, cut])


def spread_kernel(q, q_far, _, near_out, far_out):
    for j in range(near_out.shape[0]):
        near_out[j] = q[...]
        far_out[j] = q_far[...]


def merge_kernel(got, _, out, kept):
    write_message(out, *merge([got.at[j] for j in range(got.shape[0])]))


def final_kernel(got, back, out):
    numer, _, total = merge([got.at[j] for j in range(got.shape[0])] + [back])
    out[...] = (numer / total).T.astype(BF16)


def on_device(queries, new_keys, new_values, cache_k, cache_v, span_bounds, cache_len, doc_start):
    far, near, cores = (lax.axis_size(name) for name in ("far", "near", "core"))
    new, _, group, dim = queries.shape
    rows = new * group
    cache_dev = cache_k.shape[1]
    packed = cache_dev + new + (cache_dev // TILE + 1) * (dim + EXTRA)
    scale2 = math.log2(math.e) / math.sqrt(dim)

    def where():
        return (lax.axis_index("far") * near + lax.axis_index("near")) * cores + lax.axis_index("core")

    def across(x, axis):
        return lax.ppermute(x, axis, [(0, 1), (1, 0)])

    def quad(x):
        return lax.all_to_all(x, "near", split_axis=0, concat_axis=0, tiled=True)

    hbm = pl.BlockSpec(memory_space=pltpu.HBM)
    vmem = pl.BlockSpec(memory_space=pltpu.VMEM)
    smem = pl.BlockSpec(memory_space=pltpu.SMEM)
    params = pltpu.CompilerParams(vmem_limit_bytes=40 * 1024 * 1024)
    message = jax.ShapeDtypeStruct((dim + EXTRA, rows), BF16)
    dma = pltpu.SemaphoreType.DMA

    q = queries.reshape(rows, dim)
    q_far = across(q, "far")
    own = pl.pallas_call(
        functools.partial(pack_kernel, far * near * cores, where),
        out_shape=jax.ShapeDtypeStruct((packed, dim), BF16),
        in_specs=[hbm] * 4 + [smem] * 2,
        out_specs=vmem,
        scratch_shapes=[
            pltpu.VMEM((cache_dev, dim), BF16),
            pltpu.VMEM((cache_dev, dim), BF16),
            pltpu.VMEM((new, dim), BF16),
            dma,
            dma,
            dma((2,)),
        ],
        compiler_params=params,
        name="pack",
    )(cache_k, cache_v, new_keys.reshape(new, dim), new_values.reshape(new, dim), cache_len, doc_start)
    slots = jax.ShapeDtypeStruct((near, rows, dim), BF16)
    q_near, q_far = pl.pallas_call(
        spread_kernel,
        out_shape=[slots] * 2,
        in_specs=[vmem, vmem, pl.BlockSpec(memory_space=pl.ANY)],
        out_specs=[vmem] * 2,
        compiler_params=params,
        name="spread",
    )(q, q_far, own)
    q_far = quad(q_far)
    other = across(own, "core")
    q_near = quad(q_near)

    spans = span_bounds.T
    cost = pl.CostEstimate(
        flops=4 * near * rows * 2 * cache_dev * dim,
        bytes_accessed=4 << 20,
        transcendentals=near * rows * 2 * cache_dev,
    )

    def attend(blocks, away, name):
        return pl.pallas_call(
            functools.partial(attend_kernel, where, away, cache_dev, new, group, scale2),
            out_shape=jax.ShapeDtypeStruct((near,) + message.shape, BF16),
            in_specs=[smem] + [vmem] * 3,
            out_specs=vmem,
            scratch_shapes=[pltpu.VMEM((2 * cache_dev + 2 * new, WIDE), F32)] * 2
            + [pltpu.VMEM((dim + EXTRA, WIDE), F32), pltpu.VMEM((2 * new, dim), BF16), pltpu.VMEM((dim + EXTRA, TILE), BF16)],
            compiler_params=params,
            cost_estimate=cost,
            name=name,
        )(spans, own, other, blocks)

    far_out = attend(q_far, True, "far_blocks")
    far_got = quad(far_out)
    near_out = attend(q_near, False, "near_blocks")
    anywhere = pl.BlockSpec(memory_space=pl.ANY)
    far_sum, near_out = pl.pallas_call(
        merge_kernel,
        out_shape=[message, jax.ShapeDtypeStruct(near_out.shape, BF16)],
        in_specs=[vmem, anywhere],
        out_specs=[vmem, anywhere],
        input_output_aliases={1: 1},
        compiler_params=params,
        name="merge_far",
    )(far_got, near_out)
    back = across(far_sum, "far")
    near_got = quad(near_out)
    result = pl.pallas_call(
        final_kernel,
        out_shape=jax.ShapeDtypeStruct((rows, dim), BF16),
        in_specs=[vmem] * 2,
        out_specs=vmem,
        compiler_params=params,
        name="merge_all",
    )(near_got, back)
    return result.reshape(new, 1, group, dim)


def solution(mesh):
    ctx, kvh, sess = (mesh.shape[name] for name in ("ctx", "kvh", "sess"))
    devices = mesh.devices.reshape(2, ctx // 4, 2, kvh, sess)
    split = Mesh(devices, ("far", "near", "core", "kvh", "sess"))
    ctx = ("far", "near", "core")
    return jax.shard_map(
        on_device,
        mesh=split,
        in_specs=(
            P(("sess",) + ctx, "kvh", None, None),
            P(("sess",) + ctx, "kvh", None),
            P(("sess",) + ctx, "kvh", None),
            P(("sess", "kvh"), ctx, None),
            P(("sess", "kvh"), ctx, None),
            P("sess", None),
            P("sess"),
            P("sess"),
        ),
        out_specs=P(("sess",) + ctx, "kvh", None, None),
        check_vma=False,
    )
```

```python
import functools
import math

import jax
import jax.numpy as jnp
from jax import lax
from jax.experimental import pallas as pl
from jax.experimental.pallas import tpu as pltpu
from jax.sharding import Mesh
from jax.sharding import PartitionSpec as P

F32 = jnp.float32
BF16 = jnp.bfloat16
HIDDEN = -1e30
CHUNK = 1024
TILE = 128
WIDE = 512
EXTRA = 16
NT = (((1,), (1,)), ((), ()))


def pieces(x):
    hi = x.astype(BF16).astype(F32)
    mid = (x - hi).astype(BF16).astype(F32)
    return hi, mid, x - hi - mid


def write_message(out, numer, peak, total):
    dim = numer.shape[0]
    out[0:dim, :] = numer.astype(BF16)
    row = lax.broadcasted_iota(jnp.int32, (EXTRA, numer.shape[1]), 0)
    tail = jnp.zeros((EXTRA, numer.shape[1]), F32)
    for at, piece in enumerate(pieces(peak) + pieces(total)):
        tail = jnp.where(row == at, piece, tail)
    out[dim : dim + EXTRA, :] = tail.astype(BF16)


def read_message(ref):
    dim = ref.shape[0] - EXTRA
    tail = ref[dim : dim + EXTRA, :].astype(F32)
    peak = tail[0:1] + tail[1:2] + tail[2:3]
    total = tail[3:4] + tail[4:5] + tail[5:6]
    return ref[0:dim, :].astype(F32), peak, total


def merge(refs):
    parts = [read_message(ref) for ref in refs]
    peak = functools.reduce(jnp.maximum, [p[1] for p in parts])
    factors = [jnp.exp(p[1] - peak) for p in parts]
    total = sum(p[2] * f for p, f in zip(parts, factors))
    numer = sum(p[0] * f for p, f in zip(parts, factors))
    return numer, peak, total


def pack_kernel(count, where, *refs):
    k_hbm, v_hbm, nk_hbm, nv_hbm, cache_len, doc_start, pack = refs[:7]
    kbuf, vbuf, ksem, vsem, nsem = refs[7:]
    rows, dim = kbuf.shape
    new = nk_hbm.shape[0]
    base = rows + new
    me = where()
    first = lax.div(jnp.maximum(doc_start[0] - me + count - 1, 0), count)
    limit = cache_len[me]

    k_copy = pltpu.make_async_copy(k_hbm.at[0], kbuf, ksem)
    v_copy = pltpu.make_async_copy(v_hbm.at[0], vbuf, vsem)
    nk_copy = pltpu.make_async_copy(nk_hbm, pack.at[pl.ds(rows, new)], nsem.at[0])
    nv_copy = pltpu.make_async_copy(nv_hbm, pack.at[pl.ds(base + rows, new)], nsem.at[1])
    for copy in (k_copy, v_copy, nk_copy, nv_copy):
        copy.start()

    safe = rows // 8
    step = 512
    k_copy.wait()
    spare = kbuf[safe : safe + 16, :][0:1].astype(F32)
    for at in range(0, rows, step):
        slot = lax.broadcasted_iota(jnp.int32, (step, dim), 0) + at
        ok = (slot >= first) & (slot < limit)
        pack[at : at + step, :] = jnp.where(ok, kbuf[at : at + step, :].astype(F32), spare).astype(BF16)
        to = 2 * base + at
        pack[to : to + step, :] = jnp.where(ok, 1.0, 0.0).astype(BF16)
    v_copy.wait()
    for at in range(0, rows, step):
        slot = lax.broadcasted_iota(jnp.int32, (step, dim), 0) + at
        ok = (slot >= first) & (slot < limit)
        to = base + at
        pack[to : to + step, :] = jnp.where(ok, vbuf[at : at + step, :].astype(F32), 0.0).astype(BF16)
    nk_copy.wait()
    nv_copy.wait()


def fresh_mask(me, token, spans, new):
    key = lax.broadcasted_iota(jnp.int32, (token.shape[0], TILE), 1)
    real = key < 2 * new
    key = key + (me - lax.rem(me, 2)) * new
    ok = key <= token
    for k in range(spans.shape[1]):
        lo, hi = spans[0, k], spans[1, k]
        ok = ok | ((token >= lo) & (token < hi) & (key >= lo) & (key < hi))
    return ok & real


def attend(me, owners, cache_dev, new, group, scale, spans, own, other, blocks, outs, scratch):
    *s_refs, fresh_k, fresh_v = scratch
    part, dim = blocks[0].shape
    pair = WIDE // part
    n, rows = len(blocks) // pair, WIDE
    base = cache_dev + new

    odd = lax.rem(me, 2) == 1
    fill = TILE - 2 * new
    fresh = []
    for at in (cache_dev, base + cache_dev):
        mine, theirs = own[at : at + new, :].astype(F32), other[at : at + new, :].astype(F32)
        low, high = jnp.where(odd, theirs, mine), jnp.where(odd, mine, theirs)
        fresh.append(jnp.concatenate([low, high, jnp.zeros((fill, dim), F32)], axis=0))
    fresh_k[...] = fresh[0].astype(BF16)
    fresh_v[:, 0:dim] = fresh[1].astype(BF16)
    fresh_v[:, dim : 2 * dim] = jnp.ones((TILE, dim), F32).astype(BF16)

    tiles = [None] + [(which, at) for which in (0, 1) for at in range(0, cache_dev, CHUNK)]

    def place(tile):
        if tile is None:
            return slice(2 * cache_dev, 2 * cache_dev + TILE)
        start = tile[0] * cache_dev + tile[1]
        return slice(start, start + CHUNK)

    def scores(b, tile, peak):
        q = jnp.concatenate([blocks[pair * b + j][...] for j in range(pair)], axis=0)
        if tile is None:
            keys = fresh_k[...]
        else:
            which, at = tile
            keys = (own, other)[which][at : at + CHUNK, :]
        s = lax.dot_general(q, keys, NT, preferred_element_type=F32)
        if tile is None:
            inside = lax.div(lax.broadcasted_iota(jnp.int32, (part, 1), 0), group)
            token = jnp.concatenate([owners[pair * b + j] * new + inside for j in range(pair)], axis=0)
            s = jnp.where(fresh_mask(me, token, spans, new), s, HIDDEN)
        s_refs[b % 2][:, place(tile)] = s
        for j in range(s.shape[1] // TILE):
            top = s[:, j * TILE : (j + 1) * TILE]
            peak = top if peak is None else jnp.maximum(peak, top)
        return peak

    def weigh(b, tile, top, acc):
        p = jnp.exp((s_refs[b % 2][:, place(tile)] - top) * scale).astype(BF16)
        if tile is None:
            v = fresh_v[...]
        else:
            which, at = tile
            ref = (own, other)[which]
            v, m = base + at, 2 * base + at
            v = jnp.concatenate([ref[v : v + CHUNK, :], ref[m : m + CHUNK, :]], axis=1)
        o = jnp.dot(p, v, preferred_element_type=F32)
        return o if acc is None else acc + o

    peak = None
    for tile in tiles:
        peak = scores(0, tile, peak)
    lane = lax.broadcasted_iota(jnp.int32, (part, dim), 1)
    for b in range(n):
        top = jnp.max(peak, axis=1, keepdims=True)
        acc, peak = None, None
        for tile in tiles:
            acc = weigh(b, tile, top, acc)
            if b + 1 < n:
                peak = scores(b + 1, tile, peak)
        for j in range(pair):
            cut = slice(j * part, (j + 1) * part)
            both = jnp.where(lane == 0, top[cut] * scale, acc[cut, dim : 2 * dim]).T
            write_message(outs[pair * b + j], acc[cut, 0:dim].T, both[0:1], both[1:2])


def blocks_kernel(where, away, cache_dev, new, group, scale, spans, own, other, q_ref, _, out, *scratch):
    me = where()
    near = q_ref.shape[0]
    first = (me - lax.rem(me, 2 * near)) ^ (2 * near if away else 0)
    owners = [first + 2 * j + lax.rem(me, 2) for j in range(near)]
    blocks = [q_ref.at[j] for j in range(near)]
    outs = [out.at[j] for j in range(near)]
    attend(me, owners, cache_dev, new, group, scale, spans, own, other, blocks, outs, scratch)


def spread_kernel(q, _, out, kept):
    for j in range(out.shape[0]):
        out[j] = q[...]


def merge_kernel(got, _, out, kept):
    write_message(out, *merge([got.at[j] for j in range(got.shape[0])]))


def final_kernel(got, back, out):
    numer, _, total = merge([got.at[j] for j in range(got.shape[0])] + [back])
    out[...] = (numer / total).T.astype(BF16)


def on_device(queries, new_keys, new_values, cache_k, cache_v, span_bounds, cache_len, doc_start):
    far, near, cores = (lax.axis_size(name) for name in ("far", "near", "core"))
    new, _, group, dim = queries.shape
    rows = new * group
    cache_dev = cache_k.shape[1]
    packed = 3 * cache_dev + 2 * new
    scale = 1.0 / math.sqrt(dim)

    def where():
        return (lax.axis_index("far") * near + lax.axis_index("near")) * cores + lax.axis_index("core")

    def across(x, axis):
        return lax.ppermute(x, axis, [(0, 1), (1, 0)])

    def quad(x):
        return lax.all_to_all(x, "near", split_axis=0, concat_axis=0, tiled=True)

    hbm = pl.BlockSpec(memory_space=pltpu.HBM)
    vmem = pl.BlockSpec(memory_space=pltpu.VMEM)
    smem = pl.BlockSpec(memory_space=pltpu.SMEM)
    params = pltpu.CompilerParams(vmem_limit_bytes=36 * 1024 * 1024)
    message = jax.ShapeDtypeStruct((dim + EXTRA, rows), BF16)
    dma = pltpu.SemaphoreType.DMA

    q = queries.reshape(rows, dim)
    q_far = across(q, "far")
    own = pl.pallas_call(
        functools.partial(pack_kernel, far * near * cores, where),
        out_shape=jax.ShapeDtypeStruct((packed, dim), BF16),
        in_specs=[hbm] * 4 + [smem] * 2,
        out_specs=vmem,
        scratch_shapes=[
            pltpu.VMEM((cache_dev, dim), BF16),
            pltpu.VMEM((cache_dev, dim), BF16),
            dma,
            dma,
            dma((2,)),
        ],
        compiler_params=params,
        name="pack",
    )(cache_k, cache_v, new_keys.reshape(new, dim), new_values.reshape(new, dim), cache_len, doc_start)
    anywhere = pl.BlockSpec(memory_space=pl.ANY)
    q_far, own = pl.pallas_call(
        spread_kernel,
        out_shape=[jax.ShapeDtypeStruct((near, rows, dim), BF16), jax.ShapeDtypeStruct(own.shape, BF16)],
        in_specs=[vmem, anywhere],
        out_specs=[vmem, anywhere],
        input_output_aliases={1: 1},
        compiler_params=params,
        name="spread",
    )(q_far, own)
    q_far = quad(q_far)
    other = across(own, "core")
    q_near = lax.all_gather(q, "near", axis=0)

    spans = span_bounds.T
    cost = pl.CostEstimate(
        flops=4 * near * rows * 2 * cache_dev * dim,
        bytes_accessed=4 << 20,
        transcendentals=near * rows * 2 * cache_dev,
    )

    sizes = (cache_dev, new, group, scale)
    scratch = [pltpu.VMEM((WIDE, 2 * cache_dev + TILE), F32)] * 2
    scratch += [pltpu.VMEM((TILE, dim), BF16), pltpu.VMEM((TILE, 2 * dim), BF16)]
    partials = jax.ShapeDtypeStruct((near,) + message.shape, BF16)

    def attend_blocks(blocks, before, away, name):
        return pl.pallas_call(
            functools.partial(blocks_kernel, where, away, *sizes),
            out_shape=partials,
            in_specs=[smem] + [vmem] * 3 + [anywhere],
            out_specs=vmem,
            scratch_shapes=scratch,
            compiler_params=params,
            cost_estimate=cost,
            name=name,
        )(spans, own, other, blocks, before)

    far_out = attend_blocks(q_far, q_far, True, "far_blocks")
    far_got = quad(far_out)
    near_out = attend_blocks(q_near, far_out, False, "near_blocks")
    far_sum, near_out = pl.pallas_call(
        merge_kernel,
        out_shape=[message, partials],
        in_specs=[vmem, anywhere],
        out_specs=[vmem, anywhere],
        input_output_aliases={1: 1},
        compiler_params=params,
        name="merge_far",
    )(far_got, near_out)
    back = across(far_sum, "far")
    near_got = quad(near_out)
    result = pl.pallas_call(
        final_kernel,
        out_shape=jax.ShapeDtypeStruct((rows, dim), BF16),
        in_specs=[vmem] * 2,
        out_specs=vmem,
        compiler_params=params,
        name="merge_all",
    )(near_got, back)
    return result.reshape(new, 1, group, dim)


def solution(mesh):
    ctx, kvh, sess = (mesh.shape[name] for name in ("ctx", "kvh", "sess"))
    devices = mesh.devices.reshape(2, ctx // 4, 2, kvh, sess)
    split = Mesh(devices, ("far", "near", "core", "kvh", "sess"))
    ctx = ("far", "near", "core")
    return jax.shard_map(
        on_device,
        mesh=split,
        in_specs=(
            P(("sess",) + ctx, "kvh", None, None),
            P(("sess",) + ctx, "kvh", None),
            P(("sess",) + ctx, "kvh", None),
            P(("sess", "kvh"), ctx, None),
            P(("sess", "kvh"), ctx, None),
            P("sess", None),
            P("sess"),
            P("sess"),
        ),
        out_specs=P(("sess",) + ctx, "kvh", None, None),
        check_vma=False,
    )
```

```python
import functools
import math

import jax
import jax.numpy as jnp
from jax import lax
from jax.experimental import pallas as pl
from jax.experimental.pallas import tpu as pltpu
from jax.sharding import Mesh
from jax.sharding import PartitionSpec as P

F32 = jnp.float32
BF16 = jnp.bfloat16
HIDDEN = -1e30
CHUNK = 1024
TILE = 128
EXTRA = 16
NT = (((1,), (1,)), ((), ()))


def pieces(x):
    hi = x.astype(BF16).astype(F32)
    mid = (x - hi).astype(BF16).astype(F32)
    return hi, mid, x - hi - mid


def write_message(out, numer, peak, total):
    dim = numer.shape[0]
    out[0:dim, :] = numer.astype(BF16)
    row = lax.broadcasted_iota(jnp.int32, (EXTRA, numer.shape[1]), 0)
    tail = jnp.zeros((EXTRA, numer.shape[1]), F32)
    for at, piece in enumerate(pieces(peak) + pieces(total)):
        tail = jnp.where(row == at, piece, tail)
    out[dim : dim + EXTRA, :] = tail.astype(BF16)


def read_message(ref):
    dim = ref.shape[0] - EXTRA
    tail = ref[dim : dim + EXTRA, :].astype(F32)
    peak = tail[0:1] + tail[1:2] + tail[2:3]
    total = tail[3:4] + tail[4:5] + tail[5:6]
    return ref[0:dim, :].astype(F32), peak, total


def merge(refs):
    parts = [read_message(ref) for ref in refs]
    peak = functools.reduce(jnp.maximum, [p[1] for p in parts])
    factors = [jnp.exp(p[1] - peak) for p in parts]
    total = sum(p[2] * f for p, f in zip(parts, factors))
    numer = sum(p[0] * f for p, f in zip(parts, factors))
    return numer, peak, total


def pack_kernel(count, where, *refs):
    k_hbm, v_hbm, nk_hbm, nv_hbm, cache_len, doc_start, pack = refs[:7]
    kbuf, vbuf, ksem, vsem, nsem = refs[7:]
    rows, dim = kbuf.shape
    new = nk_hbm.shape[0]
    base = rows + new
    me = where()
    first = lax.div(jnp.maximum(doc_start[0] - me + count - 1, 0), count)
    limit = cache_len[me]

    k_copy = pltpu.make_async_copy(k_hbm.at[0], kbuf, ksem)
    v_copy = pltpu.make_async_copy(v_hbm.at[0], vbuf, vsem)
    nk_copy = pltpu.make_async_copy(nk_hbm, pack.at[pl.ds(rows, new)], nsem.at[0])
    nv_copy = pltpu.make_async_copy(nv_hbm, pack.at[pl.ds(base + rows, new)], nsem.at[1])
    for copy in (k_copy, v_copy, nk_copy, nv_copy):
        copy.start()

    safe = rows // 8
    step = 512
    k_copy.wait()
    spare = kbuf[safe : safe + 16, :][0:1].astype(F32)
    for at in range(0, rows, step):
        slot = lax.broadcasted_iota(jnp.int32, (step, dim), 0) + at
        ok = (slot >= first) & (slot < limit)
        pack[at : at + step, :] = jnp.where(ok, kbuf[at : at + step, :].astype(F32), spare).astype(BF16)
        to = 2 * base + at
        pack[to : to + step, :] = jnp.where(ok, 1.0, 0.0).astype(BF16)
    v_copy.wait()
    for at in range(0, rows, step):
        slot = lax.broadcasted_iota(jnp.int32, (step, dim), 0) + at
        ok = (slot >= first) & (slot < limit)
        to = base + at
        pack[to : to + step, :] = jnp.where(ok, vbuf[at : at + step, :].astype(F32), 0.0).astype(BF16)
    nk_copy.wait()
    nv_copy.wait()


def fresh_mask(me, token, spans, new):
    key = lax.broadcasted_iota(jnp.int32, (token.shape[0], TILE), 1)
    real = key < 2 * new
    key = key + (me - lax.rem(me, 2)) * new
    ok = key <= token
    for k in range(spans.shape[1]):
        lo, hi = spans[0, k], spans[1, k]
        ok = ok | ((token >= lo) & (token < hi) & (key >= lo) & (key < hi))
    return ok & real


def attend(me, owners, pair, cache_dev, new, group, scale, spans, own, other, blocks, outs, scratch):
    *s_refs, fresh_k, fresh_v = scratch
    part, dim = blocks[0].shape
    n = len(blocks) // pair
    base = cache_dev + new

    odd = lax.rem(me, 2) == 1
    fill = TILE - 2 * new
    fresh = []
    for at in (cache_dev, base + cache_dev):
        mine, theirs = own[at : at + new, :].astype(F32), other[at : at + new, :].astype(F32)
        low, high = jnp.where(odd, theirs, mine), jnp.where(odd, mine, theirs)
        fresh.append(jnp.concatenate([low, high, jnp.zeros((fill, dim), F32)], axis=0))
    fresh_k[...] = fresh[0].astype(BF16)
    fresh_v[:, 0:dim] = fresh[1].astype(BF16)
    fresh_v[:, dim : 2 * dim] = jnp.ones((TILE, dim), F32).astype(BF16)

    tiles = [None] + [(which, at) for which in (0, 1) for at in range(0, cache_dev, CHUNK)]

    def place(tile):
        if tile is None:
            return slice(2 * cache_dev, 2 * cache_dev + TILE)
        start = tile[0] * cache_dev + tile[1]
        return slice(start, start + CHUNK)

    def scores(b, tile, peak):
        q = jnp.concatenate([blocks[pair * b + j][...] for j in range(pair)], axis=0)
        if tile is None:
            keys = fresh_k[...]
        else:
            which, at = tile
            keys = (own, other)[which][at : at + CHUNK, :]
        s = lax.dot_general(q, keys, NT, preferred_element_type=F32)
        if tile is None:
            inside = lax.div(lax.broadcasted_iota(jnp.int32, (part, 1), 0), group)
            token = jnp.concatenate([owners[pair * b + j] * new + inside for j in range(pair)], axis=0)
            s = jnp.where(fresh_mask(me, token, spans, new), s, HIDDEN)
        s_refs[b % len(s_refs)][:, place(tile)] = s
        for j in range(s.shape[1] // TILE):
            top = s[:, j * TILE : (j + 1) * TILE]
            peak = top if peak is None else jnp.maximum(peak, top)
        return peak

    def weigh(b, tile, top, acc):
        p = jnp.exp((s_refs[b % len(s_refs)][:, place(tile)] - top) * scale).astype(BF16)
        if tile is None:
            v = fresh_v[...]
        else:
            which, at = tile
            ref = (own, other)[which]
            v, m = base + at, 2 * base + at
            v = jnp.concatenate([ref[v : v + CHUNK, :], ref[m : m + CHUNK, :]], axis=1)
        o = jnp.dot(p, v, preferred_element_type=F32)
        return o if acc is None else acc + o

    peak = None
    for tile in tiles:
        peak = scores(0, tile, peak)
    lane = lax.broadcasted_iota(jnp.int32, (part, dim), 1)
    for b in range(n):
        top = jnp.max(peak, axis=1, keepdims=True)
        acc, peak = None, None
        for tile in tiles:
            acc = weigh(b, tile, top, acc)
            if b + 1 < n:
                peak = scores(b + 1, tile, peak)
        for j in range(pair):
            cut = slice(j * part, (j + 1) * part)
            both = jnp.where(lane == 0, top[cut] * scale, acc[cut, dim : 2 * dim]).T
            write_message(outs[pair * b + j], acc[cut, 0:dim].T, both[0:1], both[1:2])


def own_far_kernel(where, sizes, spans, own, other, q_far, q, out, slots, *scratch):
    me = where()
    near = slots.shape[0]
    for j in range(near):
        slots[j] = q[...]
    attend(me, [me ^ (2 * near)], 1, *sizes, spans, own, other, [q_far], [out], scratch)


def far_kernel(where, sizes, spans, own, other, q_ref, mine, out, *scratch):
    me = where()
    near = q_ref.shape[0]
    at = lax.rem(lax.div(me, 2), near)
    first = (me - lax.rem(me, 2 * near)) ^ (2 * near)
    out[at] = mine[...]
    members = [lax.rem(at + j, near) for j in range(1, near)]
    owners = [first + 2 * j + lax.rem(me, 2) for j in members]
    blocks, outs = [q_ref.at[j] for j in members], [out.at[j] for j in members]
    attend(me, owners, near - 1, *sizes, spans, own, other, blocks, outs, scratch)


def near_kernel(where, sizes, spans, own, other, q_ref, _, out, *scratch):
    me = where()
    near = q_ref.shape[0]
    first = me - lax.rem(me, 2 * near)
    owners = [first + 2 * j + lax.rem(me, 2) for j in range(near)]
    blocks, outs = [q_ref.at[j] for j in range(near)], [out.at[j] for j in range(near)]
    attend(me, owners, 2, *sizes, spans, own, other, blocks, outs, scratch)


def spread_kernel(q, _, out, kept):
    for j in range(out.shape[0]):
        out[j] = q[...]


def merge_kernel(got, _, out, kept):
    write_message(out, *merge([got.at[j] for j in range(got.shape[0])]))


def final_kernel(got, back, out):
    numer, _, total = merge([got.at[j] for j in range(got.shape[0])] + [back])
    out[...] = (numer / total).T.astype(BF16)


def on_device(queries, new_keys, new_values, cache_k, cache_v, span_bounds, cache_len, doc_start):
    far, near, cores = (lax.axis_size(name) for name in ("far", "near", "core"))
    new, _, group, dim = queries.shape
    rows = new * group
    cache_dev = cache_k.shape[1]
    packed = 3 * cache_dev + 2 * new
    scale = 1.0 / math.sqrt(dim)

    def where():
        return (lax.axis_index("far") * near + lax.axis_index("near")) * cores + lax.axis_index("core")

    def across(x, axis):
        return lax.ppermute(x, axis, [(0, 1), (1, 0)])

    def quad(x):
        return lax.all_to_all(x, "near", split_axis=0, concat_axis=0, tiled=True)

    hbm = pl.BlockSpec(memory_space=pltpu.HBM)
    vmem = pl.BlockSpec(memory_space=pltpu.VMEM)
    smem = pl.BlockSpec(memory_space=pltpu.SMEM)
    params = pltpu.CompilerParams(vmem_limit_bytes=36 * 1024 * 1024)
    message = jax.ShapeDtypeStruct((dim + EXTRA, rows), BF16)
    dma = pltpu.SemaphoreType.DMA

    q = queries.reshape(rows, dim)
    q_far = across(q, "far")
    own = pl.pallas_call(
        functools.partial(pack_kernel, far * near * cores, where),
        out_shape=jax.ShapeDtypeStruct((packed, dim), BF16),
        in_specs=[hbm] * 4 + [smem] * 2,
        out_specs=vmem,
        scratch_shapes=[
            pltpu.VMEM((cache_dev, dim), BF16),
            pltpu.VMEM((cache_dev, dim), BF16),
            dma,
            dma,
            dma((2,)),
        ],
        compiler_params=params,
        name="pack",
    )(cache_k, cache_v, new_keys.reshape(new, dim), new_values.reshape(new, dim), cache_len, doc_start)
    anywhere = pl.BlockSpec(memory_space=pl.ANY)
    q_slots, own = pl.pallas_call(
        spread_kernel,
        out_shape=[jax.ShapeDtypeStruct((near, rows, dim), BF16), jax.ShapeDtypeStruct(own.shape, BF16)],
        in_specs=[vmem, anywhere],
        out_specs=[vmem, anywhere],
        input_output_aliases={1: 1},
        compiler_params=params,
        name="spread",
    )(q_far, own)
    q_slots = quad(q_slots)
    other = across(own, "core")

    spans = span_bounds.T
    sizes = (cache_dev, new, group, scale)
    partials = jax.ShapeDtypeStruct((near,) + message.shape, BF16)

    def attend_call(kernel, last, out_shape, unit, count, name):
        return pl.pallas_call(
            functools.partial(kernel, where, sizes),
            out_shape=out_shape,
            in_specs=[smem] + [vmem] * 3 + [last],
            out_specs=jax.tree.map(lambda _: vmem, out_shape),
            scratch_shapes=[pltpu.VMEM((unit * rows, 2 * cache_dev + TILE), F32)] * (count // unit)
            + [pltpu.VMEM((TILE, dim), BF16), pltpu.VMEM((TILE, 2 * dim), BF16)],
            compiler_params=params,
            cost_estimate=pl.CostEstimate(
                flops=4 * count * rows * 2 * cache_dev * dim,
                bytes_accessed=4 << 20,
                transcendentals=count * rows * 2 * cache_dev,
            ),
            name=name,
        )

    slots = jax.ShapeDtypeStruct((near, rows, dim), BF16)
    own_far, near_slots = attend_call(own_far_kernel, vmem, [message, slots], 1, 1, "own_far")(spans, own, other, q_far, q)
    q_near = quad(near_slots)
    far_out = attend_call(far_kernel, vmem, partials, near - 1, near - 1, "far_blocks")(
        spans, own, other, q_slots, own_far
    )
    far_got = quad(far_out)
    near_out = attend_call(near_kernel, anywhere, partials, 2, near, "near_blocks")(spans, own, other, q_near, far_out)
    far_sum, near_out = pl.pallas_call(
        merge_kernel,
        out_shape=[message, partials],
        in_specs=[vmem, anywhere],
        out_specs=[vmem, anywhere],
        input_output_aliases={1: 1},
        compiler_params=params,
        name="merge_far",
    )(far_got, near_out)
    back = across(far_sum, "far")
    near_got = quad(near_out)
    result = pl.pallas_call(
        final_kernel,
        out_shape=jax.ShapeDtypeStruct((rows, dim), BF16),
        in_specs=[vmem] * 2,
        out_specs=vmem,
        compiler_params=params,
        name="merge_all",
    )(near_got, back)
    return result.reshape(new, 1, group, dim)


def solution(mesh):
    ctx, kvh, sess = (mesh.shape[name] for name in ("ctx", "kvh", "sess"))
    devices = mesh.devices.reshape(2, ctx // 4, 2, kvh, sess)
    split = Mesh(devices, ("far", "near", "core", "kvh", "sess"))
    ctx = ("far", "near", "core")
    return jax.shard_map(
        on_device,
        mesh=split,
        in_specs=(
            P(("sess",) + ctx, "kvh", None, None),
            P(("sess",) + ctx, "kvh", None),
            P(("sess",) + ctx, "kvh", None),
            P(("sess", "kvh"), ctx, None),
            P(("sess", "kvh"), ctx, None),
            P("sess", None),
            P("sess"),
            P("sess"),
        ),
        out_specs=P(("sess",) + ctx, "kvh", None, None),
        check_vma=False,
    )
```

```python
import functools
import math

import jax
import jax.numpy as jnp
from jax import lax
from jax.experimental import pallas as pl
from jax.experimental.pallas import tpu as pltpu
from jax.sharding import Mesh
from jax.sharding import PartitionSpec as P

F32 = jnp.float32
BF16 = jnp.bfloat16
HIDDEN = -1e30
CHUNK = 1024
TILE = 128
WIDE = 512
EXTRA = 16
NT = (((1,), (1,)), ((), ()))


def pieces(x):
    hi = x.astype(BF16).astype(F32)
    mid = (x - hi).astype(BF16).astype(F32)
    return hi, mid, x - hi - mid


def write_message(out, numer, peak, total):
    dim = numer.shape[0]
    out[0:dim, :] = numer.astype(BF16)
    row = lax.broadcasted_iota(jnp.int32, (EXTRA, numer.shape[1]), 0)
    tail = jnp.zeros((EXTRA, numer.shape[1]), F32)
    for at, piece in enumerate(pieces(peak) + pieces(total)):
        tail = jnp.where(row == at, piece, tail)
    out[dim : dim + EXTRA, :] = tail.astype(BF16)


def read_message(ref):
    dim = ref.shape[0] - EXTRA
    tail = ref[dim : dim + EXTRA, :].astype(F32)
    peak = tail[0:1] + tail[1:2] + tail[2:3]
    total = tail[3:4] + tail[4:5] + tail[5:6]
    return ref[0:dim, :].astype(F32), peak, total


def merge(refs):
    parts = [read_message(ref) for ref in refs]
    peak = functools.reduce(jnp.maximum, [p[1] for p in parts])
    factors = [jnp.exp2(p[1] - peak) for p in parts]
    total = sum(p[2] * f for p, f in zip(parts, factors))
    numer = sum(p[0] * f for p, f in zip(parts, factors))
    return numer, peak, total


def pack_kernel(count, where, *refs):
    k_hbm, v_hbm, nk_hbm, nv_hbm, cache_len, doc_start, pack = refs[:7]
    kbuf, vbuf, nvbuf, ksem, vsem, nsem = refs[7:]
    rows, dim = kbuf.shape
    new = nvbuf.shape[0]
    me = where()
    first = lax.div(jnp.maximum(doc_start[0] - me + count - 1, 0), count)
    limit = cache_len[me]

    k_copy = pltpu.make_async_copy(k_hbm.at[0], kbuf, ksem)
    v_copy = pltpu.make_async_copy(v_hbm.at[0], vbuf, vsem)
    nk_copy = pltpu.make_async_copy(nk_hbm, pack.at[pl.ds(rows, new)], nsem.at[0])
    nv_copy = pltpu.make_async_copy(nv_hbm, nvbuf, nsem.at[1])
    copies = [nk_copy, nv_copy]
    for copy in [k_copy, v_copy, *copies]:
        copy.start()

    safe = rows // 8
    step = 4 * TILE
    base = rows + new
    k_copy.wait()
    spare = kbuf[safe : safe + 16, :][0:1].astype(F32)
    for at in range(0, rows, step):
        slot = lax.broadcasted_iota(jnp.int32, (step, dim), 0) + at
        ok = (slot >= first) & (slot < limit)
        pack[at : at + step, :] = jnp.where(ok, kbuf[at : at + step, :].astype(F32), spare).astype(BF16)
    v_copy.wait()
    for at in range(0, rows, TILE):
        to = base + at // TILE * (dim + EXTRA)
        slot = lax.broadcasted_iota(jnp.int32, (TILE, dim), 0) + at
        ok = (slot >= first) & (slot < limit)
        values = jnp.where(ok, vbuf[at : at + TILE, :].astype(F32), 0.0)
        pack[to : to + dim, :] = values.T.astype(BF16)
        slot = lax.broadcasted_iota(jnp.int32, (EXTRA, TILE), 1) + at
        row = lax.broadcasted_iota(jnp.int32, (EXTRA, TILE), 0)
        ok = (slot >= first) & (slot < limit) & (row == 0)
        pack[to + dim : to + dim + EXTRA, :] = jnp.where(ok, 1.0, 0.0).astype(BF16)
    for copy in copies:
        copy.wait()
    to = base + rows // TILE * (dim + EXTRA)
    odd = lax.rem(me, 2) == 1
    own = nvbuf[...].astype(F32)
    none = jnp.zeros_like(own)
    both = [jnp.where(odd, none, own), jnp.where(odd, own, none), jnp.zeros((TILE - 2 * new, dim), F32)]
    pack[to : to + dim, :] = jnp.concatenate(both, axis=0).T.astype(BF16)
    row = lax.broadcasted_iota(jnp.int32, (EXTRA, TILE), 0)
    column = lax.broadcasted_iota(jnp.int32, (EXTRA, TILE), 1)
    mine = lax.div(column, new) == lax.rem(me, 2)
    pack[to + dim : to + dim + EXTRA, :] = jnp.where((row == 0) & mine, 1.0, 0.0).astype(BF16)


def fresh_mask(me, token, spans, new):
    key = lax.broadcasted_iota(jnp.int32, (2 * new, token.shape[1]), 0) + (me - lax.rem(me, 2)) * new
    ok = key <= token
    for k in range(spans.shape[1]):
        lo, hi = spans[0, k], spans[1, k]
        ok = ok | ((token >= lo) & (token < hi) & (key >= lo) & (key < hi))
    return ok


def attend_kernel(where, away, cache_dev, new, group, scale2, spans, own, other, q_ref, out, s0, s1, fresh_k, fresh_v):
    members, part, dim = q_ref.shape
    pair = WIDE // part
    n, rows = members // pair, WIDE
    me = where()
    core = lax.rem(me, 2)
    quad = (me - lax.rem(me, 2 * members)) ^ (2 * members if away else 0)
    base = cache_dev + new
    tall = dim + EXTRA
    s_refs = (s0, s1)

    odd = core == 1
    mine, theirs = own[cache_dev:base, :].astype(F32), other[cache_dev:base, :].astype(F32)
    fresh_k[0:new, :] = jnp.where(odd, theirs, mine).astype(BF16)
    fresh_k[new : 2 * new, :] = jnp.where(odd, mine, theirs).astype(BF16)
    at = base + cache_dev // TILE * tall
    fresh_v[...] = (own[at : at + tall, :].astype(F32) + other[at : at + tall, :].astype(F32)).astype(BF16)

    tiles = [(which, at) for which in (0, 1) for at in range(0, cache_dev, CHUNK)] + [None]

    def block(b):
        return q_ref[pair * b : pair * (b + 1)].reshape(rows, dim)

    def scores(b, tile, peak):
        if tile is None:
            s = lax.dot_general(fresh_k[...], block(b), NT, preferred_element_type=F32)
            lane = lax.broadcasted_iota(jnp.int32, (1, rows), 1)
            owner = quad + (pair * b + lax.div(lane, part)) * 2 + core
            token = owner * new + lax.div(lax.rem(lane, part), group)
            s = jnp.where(fresh_mask(me, token, spans, new), s, HIDDEN)
            to, size = 2 * cache_dev, 2 * new
        else:
            which, at = tile
            s = lax.dot_general((own, other)[which][at : at + CHUNK, :], block(b), NT, preferred_element_type=F32)
            to, size = which * cache_dev + at, CHUNK
        s_refs[b % 2][to : to + size, :] = s
        top = jnp.max(s.reshape(size // 8, 8, rows), axis=0)
        return top if peak is None else jnp.maximum(peak, top)

    def weigh(b, tile, peak, acc):
        if tile is None:
            s = s_refs[b % 2][2 * cache_dev : 2 * cache_dev + 2 * new, :]
            p = jnp.exp2((s - peak) * scale2)
            p = jnp.concatenate([p, jnp.zeros((TILE - 2 * new, rows), F32)], axis=0).astype(BF16)
            v = fresh_v[...]
        else:
            which, at = tile
            to = which * cache_dev + at
            p = jnp.exp2((s_refs[b % 2][to : to + CHUNK, :] - peak) * scale2).astype(BF16)
            starts = [base + (at // TILE + j) * tall for j in range(CHUNK // TILE)]
            v = jnp.concatenate([(own, other)[which][i : i + tall, :] for i in starts], axis=1)
        o = jnp.dot(v, p, preferred_element_type=F32)
        return o if acc is None else acc + o

    peak = None
    for tile in tiles:
        peak = scores(0, tile, peak)
    for b in range(n):
        top = jnp.max(peak, axis=0, keepdims=True)
        acc, peak = None, None
        for tile in tiles:
            acc = weigh(b, tile, top, acc)
            if b + 1 < n:
                peak = scores(b + 1, tile, peak)
        for j in range(pair):
            cut = slice(j * part, (j + 1) * part)
            write_message(out.at[pair * b + j], acc[0:dim, cut], top[:, cut] * scale2, acc[dim : dim + 1, cut])


def spread_kernel(q, q_far, _, near_out, far_out):
    for j in range(near_out.shape[0]):
        near_out[j] = q[...]
        far_out[j] = q_far[...]


def merge_kernel(got, _, out, kept):
    write_message(out, *merge([got.at[j] for j in range(got.shape[0])]))


def final_kernel(got, back, out):
    numer, _, total = merge([got.at[j] for j in range(got.shape[0])] + [back])
    out[...] = (numer / total).T.astype(BF16)


def on_device(queries, new_keys, new_values, cache_k, cache_v, span_bounds, cache_len, doc_start):
    far, near, cores = (lax.axis_size(name) for name in ("far", "near", "core"))
    new, _, group, dim = queries.shape
    rows = new * group
    cache_dev = cache_k.shape[1]
    packed = cache_dev + new + (cache_dev // TILE + 1) * (dim + EXTRA)
    scale2 = math.log2(math.e) / math.sqrt(dim)

    def where():
        return (lax.axis_index("far") * near + lax.axis_index("near")) * cores + lax.axis_index("core")

    def across(x, axis):
        return lax.ppermute(x, axis, [(0, 1), (1, 0)])

    def quad(x):
        return lax.all_to_all(x, "near", split_axis=0, concat_axis=0, tiled=True)

    hbm = pl.BlockSpec(memory_space=pltpu.HBM)
    vmem = pl.BlockSpec(memory_space=pltpu.VMEM)
    smem = pl.BlockSpec(memory_space=pltpu.SMEM)
    params = pltpu.CompilerParams(vmem_limit_bytes=40 * 1024 * 1024)
    message = jax.ShapeDtypeStruct((dim + EXTRA, rows), BF16)
    dma = pltpu.SemaphoreType.DMA

    q = queries.reshape(rows, dim)
    q_far = across(q, "far")
    own = pl.pallas_call(
        functools.partial(pack_kernel, far * near * cores, where),
        out_shape=jax.ShapeDtypeStruct((packed, dim), BF16),
        in_specs=[hbm] * 4 + [smem] * 2,
        out_specs=vmem,
        scratch_shapes=[
            pltpu.VMEM((cache_dev, dim), BF16),
            pltpu.VMEM((cache_dev, dim), BF16),
            pltpu.VMEM((new, dim), BF16),
            dma,
            dma,
            dma((2,)),
        ],
        compiler_params=params,
        name="pack",
    )(cache_k, cache_v, new_keys.reshape(new, dim), new_values.reshape(new, dim), cache_len, doc_start)
    slots = jax.ShapeDtypeStruct((near, rows, dim), BF16)
    q_near, q_far = pl.pallas_call(
        spread_kernel,
        out_shape=[slots] * 2,
        in_specs=[vmem, vmem, pl.BlockSpec(memory_space=pl.ANY)],
        out_specs=[vmem] * 2,
        compiler_params=params,
        name="spread",
    )(q, q_far, own)
    q_far = quad(q_far)
    other = across(own, "core")
    q_near = quad(q_near)

    spans = span_bounds.T
    cost = pl.CostEstimate(
        flops=4 * near * rows * 2 * cache_dev * dim,
        bytes_accessed=4 << 20,
        transcendentals=near * rows * 2 * cache_dev,
    )

    def attend(blocks, away, name):
        return pl.pallas_call(
            functools.partial(attend_kernel, where, away, cache_dev, new, group, scale2),
            out_shape=jax.ShapeDtypeStruct((near,) + message.shape, BF16),
            in_specs=[smem] + [vmem] * 3,
            out_specs=vmem,
            scratch_shapes=[pltpu.VMEM((2 * cache_dev + 2 * new, WIDE), F32)] * 2
            + [pltpu.VMEM((2 * new, dim), BF16), pltpu.VMEM((dim + EXTRA, TILE), BF16)],
            compiler_params=params,
            cost_estimate=cost,
            name=name,
        )(spans, own, other, blocks)

    far_out = attend(q_far, True, "far_blocks")
    far_got = quad(far_out)
    near_out = attend(q_near, False, "near_blocks")
    anywhere = pl.BlockSpec(memory_space=pl.ANY)
    far_sum, near_out = pl.pallas_call(
        merge_kernel,
        out_shape=[message, jax.ShapeDtypeStruct(near_out.shape, BF16)],
        in_specs=[vmem, anywhere],
        out_specs=[vmem, anywhere],
        input_output_aliases={1: 1},
        compiler_params=params,
        name="merge_far",
    )(far_got, near_out)
    back = across(far_sum, "far")
    near_got = quad(near_out)
    result = pl.pallas_call(
        final_kernel,
        out_shape=jax.ShapeDtypeStruct((rows, dim), BF16),
        in_specs=[vmem] * 2,
        out_specs=vmem,
        compiler_params=params,
        name="merge_all",
    )(near_got, back)
    return result.reshape(new, 1, group, dim)


def solution(mesh):
    ctx, kvh, sess = (mesh.shape[name] for name in ("ctx", "kvh", "sess"))
    devices = mesh.devices.reshape(2, ctx // 4, 2, kvh, sess)
    split = Mesh(devices, ("far", "near", "core", "kvh", "sess"))
    ctx = ("far", "near", "core")
    return jax.shard_map(
        on_device,
        mesh=split,
        in_specs=(
            P(("sess",) + ctx, "kvh", None, None),
            P(("sess",) + ctx, "kvh", None),
            P(("sess",) + ctx, "kvh", None),
            P(("sess", "kvh"), ctx, None),
            P(("sess", "kvh"), ctx, None),
            P("sess", None),
            P("sess"),
            P("sess"),
        ),
        out_specs=P(("sess",) + ctx, "kvh", None, None),
        check_vma=False,
    )
```

```python
import functools
import math

import jax
import jax.numpy as jnp
from jax import lax
from jax.experimental import pallas as pl
from jax.experimental.pallas import tpu as pltpu
from jax.sharding import Mesh
from jax.sharding import PartitionSpec as P

F32 = jnp.float32
BF16 = jnp.bfloat16
HIDDEN = -1e30
CHUNK = 1024
TILE = 128
WIDE = 512
EXTRA = 16
NT = (((1,), (1,)), ((), ()))


def pieces(x):
    hi = x.astype(BF16).astype(F32)
    mid = (x - hi).astype(BF16).astype(F32)
    return hi, mid, x - hi - mid


def write_message(out, numer, peak, total):
    dim = numer.shape[0]
    out[0:dim, :] = numer.astype(BF16)
    row = lax.broadcasted_iota(jnp.int32, (EXTRA, numer.shape[1]), 0)
    tail = jnp.zeros((EXTRA, numer.shape[1]), F32)
    for at, piece in enumerate(pieces(peak) + pieces(total)):
        tail = jnp.where(row == at, piece, tail)
    out[dim : dim + EXTRA, :] = tail.astype(BF16)


def read_message(ref):
    dim = ref.shape[0] - EXTRA
    tail = ref[dim : dim + EXTRA, :].astype(F32)
    peak = tail[0:1] + tail[1:2] + tail[2:3]
    total = tail[3:4] + tail[4:5] + tail[5:6]
    return ref[0:dim, :].astype(F32), peak, total


def merge(refs):
    parts = [read_message(ref) for ref in refs]
    peak = functools.reduce(jnp.maximum, [p[1] for p in parts])
    factors = [jnp.exp2(p[1] - peak) for p in parts]
    total = sum(p[2] * f for p, f in zip(parts, factors))
    numer = sum(p[0] * f for p, f in zip(parts, factors))
    return numer, peak, total


def pack_kernel(count, where, *refs):
    k_hbm, v_hbm, nk_hbm, nv_hbm, cache_len, doc_start, pack = refs[:7]
    kbuf, vbuf, nvbuf, ksem, vsem, nsem = refs[7:]
    rows, dim = kbuf.shape
    new = nvbuf.shape[0]
    me = where()
    first = lax.div(jnp.maximum(doc_start[0] - me + count - 1, 0), count)
    limit = cache_len[me]

    k_copy = pltpu.make_async_copy(k_hbm.at[0], kbuf, ksem)
    v_copy = pltpu.make_async_copy(v_hbm.at[0], vbuf, vsem)
    nk_copy = pltpu.make_async_copy(nk_hbm, pack.at[pl.ds(rows, new)], nsem.at[0])
    nv_copy = pltpu.make_async_copy(nv_hbm, nvbuf, nsem.at[1])
    copies = [nk_copy, nv_copy]
    for copy in [k_copy, v_copy, *copies]:
        copy.start()

    safe = rows // 8
    step = 4 * TILE
    base = rows + new
    k_copy.wait()
    spare = kbuf[safe : safe + 16, :][0:1].astype(F32)
    for at in range(0, rows, step):
        slot = lax.broadcasted_iota(jnp.int32, (step, dim), 0) + at
        ok = (slot >= first) & (slot < limit)
        pack[at : at + step, :] = jnp.where(ok, kbuf[at : at + step, :].astype(F32), spare).astype(BF16)
    v_copy.wait()
    for at in range(0, rows, TILE):
        to = base + at // TILE * (dim + EXTRA)
        slot = lax.broadcasted_iota(jnp.int32, (TILE, dim), 0) + at
        ok = (slot >= first) & (slot < limit)
        values = jnp.where(ok, vbuf[at : at + TILE, :].astype(F32), 0.0)
        pack[to : to + dim, :] = values.T.astype(BF16)
        slot = lax.broadcasted_iota(jnp.int32, (EXTRA, TILE), 1) + at
        row = lax.broadcasted_iota(jnp.int32, (EXTRA, TILE), 0)
        ok = (slot >= first) & (slot < limit) & (row == 0)
        pack[to + dim : to + dim + EXTRA, :] = jnp.where(ok, 1.0, 0.0).astype(BF16)
    for copy in copies:
        copy.wait()
    to = base + rows // TILE * (dim + EXTRA)
    odd = lax.rem(me, 2) == 1
    own = nvbuf[...].astype(F32)
    none = jnp.zeros_like(own)
    both = [jnp.where(odd, none, own), jnp.where(odd, own, none), jnp.zeros((TILE - 2 * new, dim), F32)]
    pack[to : to + dim, :] = jnp.concatenate(both, axis=0).T.astype(BF16)
    row = lax.broadcasted_iota(jnp.int32, (EXTRA, TILE), 0)
    column = lax.broadcasted_iota(jnp.int32, (EXTRA, TILE), 1)
    mine = lax.div(column, new) == lax.rem(me, 2)
    pack[to + dim : to + dim + EXTRA, :] = jnp.where((row == 0) & mine, 1.0, 0.0).astype(BF16)


def fresh_mask(me, token, spans, new):
    key = lax.broadcasted_iota(jnp.int32, (2 * new, token.shape[1]), 0) + (me - lax.rem(me, 2)) * new
    ok = key <= token
    for k in range(spans.shape[1]):
        lo, hi = spans[0, k], spans[1, k]
        ok = ok | ((token >= lo) & (token < hi) & (key >= lo) & (key < hi))
    return ok


def attend_kernel(where, away, cache_dev, new, group, scale2, spans, own, other, q_ref, out, s0, s1, fresh_k, fresh_v):
    members, part, dim = q_ref.shape
    pair = WIDE // part
    n, rows = members // pair, WIDE
    me = where()
    core = lax.rem(me, 2)
    quad = (me - lax.rem(me, 2 * members)) ^ (2 * members if away else 0)
    base = cache_dev + new
    tall = dim + EXTRA
    s_refs = (s0, s1)

    odd = core == 1
    mine, theirs = own[cache_dev:base, :].astype(F32), other[cache_dev:base, :].astype(F32)
    fresh_k[0:new, :] = jnp.where(odd, theirs, mine).astype(BF16)
    fresh_k[new : 2 * new, :] = jnp.where(odd, mine, theirs).astype(BF16)
    at = base + cache_dev // TILE * tall
    fresh_v[...] = (own[at : at + tall, :].astype(F32) + other[at : at + tall, :].astype(F32)).astype(BF16)

    tiles = [(which, at) for which in (0, 1) for at in range(0, cache_dev, CHUNK)] + [None]

    def block(b):
        return q_ref[pair * b : pair * (b + 1)].reshape(rows, dim)

    def scores(b, tile, peak):
        if tile is None:
            s = lax.dot_general(fresh_k[...], block(b), NT, preferred_element_type=F32)
            lane = lax.broadcasted_iota(jnp.int32, (1, rows), 1)
            owner = quad + (pair * b + lax.div(lane, part)) * 2 + core
            token = owner * new + lax.div(lax.rem(lane, part), group)
            s = jnp.where(fresh_mask(me, token, spans, new), s, HIDDEN)
            to, size = 2 * cache_dev, 2 * new
        else:
            which, at = tile
            s = lax.dot_general((own, other)[which][at : at + CHUNK, :], block(b), NT, preferred_element_type=F32)
            to, size = which * cache_dev + at, CHUNK
        s_refs[b % 2][to : to + size, :] = s
        top = jnp.max(s.reshape(size // 8, 8, rows), axis=0)
        return top if peak is None else jnp.maximum(peak, top)

    def weigh(b, tile, peak, acc):
        if tile is None:
            s = s_refs[b % 2][2 * cache_dev : 2 * cache_dev + 2 * new, :]
            p = jnp.exp2((s - peak) * scale2)
            p = jnp.concatenate([p, jnp.zeros((TILE - 2 * new, rows), F32)], axis=0).astype(BF16)
            v = fresh_v[...]
        else:
            which, at = tile
            to = which * cache_dev + at
            p = jnp.exp2((s_refs[b % 2][to : to + CHUNK, :] - peak) * scale2).astype(BF16)
            starts = [base + (at // TILE + j) * tall for j in range(CHUNK // TILE)]
            v = jnp.concatenate([(own, other)[which][i : i + tall, :] for i in starts], axis=1)
        o = jnp.dot(v, p, preferred_element_type=F32)
        return o if acc is None else acc + o

    peak = None
    for tile in tiles:
        peak = scores(0, tile, peak)
    for b in range(n):
        top = jnp.max(peak, axis=0, keepdims=True)
        acc, peak = None, None
        for tile in tiles:
            acc = weigh(b, tile, top, acc)
            if b + 1 < n:
                peak = scores(b + 1, tile, peak)
        for j in range(pair):
            cut = slice(j * part, (j + 1) * part)
            write_message(out.at[pair * b + j], acc[0:dim, cut], top[:, cut] * scale2, acc[dim : dim + 1, cut])


def spread_kernel(q, _, out):
    for j in range(out.shape[0]):
        out[j] = q[...]


def merge_kernel(got, _, out, kept):
    write_message(out, *merge([got.at[j] for j in range(got.shape[0])]))


def final_kernel(got, back, out):
    numer, _, total = merge([got.at[j] for j in range(got.shape[0])] + [back])
    out[...] = (numer / total).T.astype(BF16)


def on_device(queries, new_keys, new_values, cache_k, cache_v, span_bounds, cache_len, doc_start):
    far, near, cores = (lax.axis_size(name) for name in ("far", "near", "core"))
    new, _, group, dim = queries.shape
    rows = new * group
    cache_dev = cache_k.shape[1]
    packed = cache_dev + new + (cache_dev // TILE + 1) * (dim + EXTRA)
    scale2 = math.log2(math.e) / math.sqrt(dim)

    def where():
        return (lax.axis_index("far") * near + lax.axis_index("near")) * cores + lax.axis_index("core")

    def across(x, axis):
        return lax.ppermute(x, axis, [(0, 1), (1, 0)])

    def quad(x):
        return lax.all_to_all(x, "near", split_axis=0, concat_axis=0, tiled=True)

    hbm = pl.BlockSpec(memory_space=pltpu.HBM)
    vmem = pl.BlockSpec(memory_space=pltpu.VMEM)
    smem = pl.BlockSpec(memory_space=pltpu.SMEM)
    params = pltpu.CompilerParams(vmem_limit_bytes=40 * 1024 * 1024)
    message = jax.ShapeDtypeStruct((dim + EXTRA, rows), BF16)
    dma = pltpu.SemaphoreType.DMA

    q = queries.reshape(rows, dim)
    q_far = across(q, "far")
    own = pl.pallas_call(
        functools.partial(pack_kernel, far * near * cores, where),
        out_shape=jax.ShapeDtypeStruct((packed, dim), BF16),
        in_specs=[hbm] * 4 + [smem] * 2,
        out_specs=vmem,
        scratch_shapes=[
            pltpu.VMEM((cache_dev, dim), BF16),
            pltpu.VMEM((cache_dev, dim), BF16),
            pltpu.VMEM((new, dim), BF16),
            dma,
            dma,
            dma((2,)),
        ],
        compiler_params=params,
        name="pack",
    )(cache_k, cache_v, new_keys.reshape(new, dim), new_values.reshape(new, dim), cache_len, doc_start)
    def spread(block, before, name):
        return pl.pallas_call(
            spread_kernel,
            out_shape=jax.ShapeDtypeStruct((near, rows, dim), BF16),
            in_specs=[vmem, pl.BlockSpec(memory_space=pl.ANY)],
            out_specs=vmem,
            compiler_params=params,
            name=name,
        )(block, before)

    q_far = spread(q_far, own, "spread_far")
    q_near = spread(q, q_far, "spread_near")
    q_far = quad(q_far)
    other = across(own, "core")
    q_near = quad(q_near)

    spans = span_bounds.T
    cost = pl.CostEstimate(
        flops=4 * near * rows * 2 * cache_dev * dim,
        bytes_accessed=4 << 20,
        transcendentals=near * rows * 2 * cache_dev,
    )

    def attend(blocks, away, name):
        return pl.pallas_call(
            functools.partial(attend_kernel, where, away, cache_dev, new, group, scale2),
            out_shape=jax.ShapeDtypeStruct((near,) + message.shape, BF16),
            in_specs=[smem] + [vmem] * 3,
            out_specs=vmem,
            scratch_shapes=[pltpu.VMEM((2 * cache_dev + 2 * new, WIDE), F32)] * 2
            + [pltpu.VMEM((2 * new, dim), BF16), pltpu.VMEM((dim + EXTRA, TILE), BF16)],
            compiler_params=params,
            cost_estimate=cost,
            name=name,
        )(spans, own, other, blocks)

    far_out = attend(q_far, True, "far_blocks")
    far_got = quad(far_out)
    near_out = attend(q_near, False, "near_blocks")
    anywhere = pl.BlockSpec(memory_space=pl.ANY)
    far_sum, near_out = pl.pallas_call(
        merge_kernel,
        out_shape=[message, jax.ShapeDtypeStruct(near_out.shape, BF16)],
        in_specs=[vmem, anywhere],
        out_specs=[vmem, anywhere],
        input_output_aliases={1: 1},
        compiler_params=params,
        name="merge_far",
    )(far_got, near_out)
    back = across(far_sum, "far")
    near_got = quad(near_out)
    result = pl.pallas_call(
        final_kernel,
        out_shape=jax.ShapeDtypeStruct((rows, dim), BF16),
        in_specs=[vmem] * 2,
        out_specs=vmem,
        compiler_params=params,
        name="merge_all",
    )(near_got, back)
    return result.reshape(new, 1, group, dim)


def solution(mesh):
    ctx, kvh, sess = (mesh.shape[name] for name in ("ctx", "kvh", "sess"))
    devices = mesh.devices.reshape(2, ctx // 4, 2, kvh, sess)
    split = Mesh(devices, ("far", "near", "core", "kvh", "sess"))
    ctx = ("far", "near", "core")
    return jax.shard_map(
        on_device,
        mesh=split,
        in_specs=(
            P(("sess",) + ctx, "kvh", None, None),
            P(("sess",) + ctx, "kvh", None),
            P(("sess",) + ctx, "kvh", None),
            P(("sess", "kvh"), ctx, None),
            P(("sess", "kvh"), ctx, None),
            P("sess", None),
            P("sess"),
            P("sess"),
        ),
        out_specs=P(("sess",) + ctx, "kvh", None, None),
        check_vma=False,
    )
```

```python
import functools
import math

import jax
import jax.numpy as jnp
from jax import lax
from jax.experimental import pallas as pl
from jax.experimental.pallas import tpu as pltpu
from jax.sharding import Mesh
from jax.sharding import PartitionSpec as P

F32 = jnp.float32
BF16 = jnp.bfloat16
HIDDEN = -1e30
CHUNK = 2048
TILE = 128
WIDE = 512
EXTRA = 16
NT = (((1,), (1,)), ((), ()))


def pieces(x):
    hi = x.astype(BF16).astype(F32)
    mid = (x - hi).astype(BF16).astype(F32)
    return hi, mid, x - hi - mid


def write_message(out, numer, peak, total):
    dim = numer.shape[0]
    out[0:dim, :] = numer.astype(BF16)
    row = lax.broadcasted_iota(jnp.int32, (EXTRA, numer.shape[1]), 0)
    tail = jnp.zeros((EXTRA, numer.shape[1]), F32)
    for at, piece in enumerate(pieces(peak) + pieces(total)):
        tail = jnp.where(row == at, piece, tail)
    out[dim : dim + EXTRA, :] = tail.astype(BF16)


def read_message(ref):
    dim = ref.shape[0] - EXTRA
    tail = ref[dim : dim + EXTRA, :].astype(F32)
    peak = tail[0:1] + tail[1:2] + tail[2:3]
    total = tail[3:4] + tail[4:5] + tail[5:6]
    return ref[0:dim, :].astype(F32), peak, total


def merge(refs):
    parts = [read_message(ref) for ref in refs]
    peak = functools.reduce(jnp.maximum, [p[1] for p in parts])
    factors = [jnp.exp2(p[1] - peak) for p in parts]
    total = sum(p[2] * f for p, f in zip(parts, factors))
    numer = sum(p[0] * f for p, f in zip(parts, factors))
    return numer, peak, total


def pack_kernel(count, where, *refs):
    k_hbm, v_hbm, nk_hbm, nv_hbm, cache_len, doc_start, pack = refs[:7]
    kbuf, vbuf, nvbuf, ksem, vsem, nsem = refs[7:]
    rows, dim = kbuf.shape
    new = nvbuf.shape[0]
    me = where()
    first = lax.div(jnp.maximum(doc_start[0] - me + count - 1, 0), count)
    limit = cache_len[me]

    k_copy = pltpu.make_async_copy(k_hbm.at[0], kbuf, ksem)
    v_copy = pltpu.make_async_copy(v_hbm.at[0], vbuf, vsem)
    nk_copy = pltpu.make_async_copy(nk_hbm, pack.at[pl.ds(rows, new)], nsem.at[0])
    nv_copy = pltpu.make_async_copy(nv_hbm, nvbuf, nsem.at[1])
    copies = [nk_copy, nv_copy]
    for copy in [k_copy, v_copy, *copies]:
        copy.start()

    safe = rows // 8
    step = 4 * TILE
    base = rows + new
    k_copy.wait()
    spare = kbuf[safe : safe + 16, :][0:1].astype(F32)
    for at in range(0, rows, step):
        slot = lax.broadcasted_iota(jnp.int32, (step, dim), 0) + at
        ok = (slot >= first) & (slot < limit)
        pack[at : at + step, :] = jnp.where(ok, kbuf[at : at + step, :].astype(F32), spare).astype(BF16)
    v_copy.wait()
    for at in range(0, rows, TILE):
        to = base + at // TILE * (dim + EXTRA)
        slot = lax.broadcasted_iota(jnp.int32, (TILE, dim), 0) + at
        ok = (slot >= first) & (slot < limit)
        values = jnp.where(ok, vbuf[at : at + TILE, :].astype(F32), 0.0)
        pack[to : to + dim, :] = values.T.astype(BF16)
        slot = lax.broadcasted_iota(jnp.int32, (EXTRA, TILE), 1) + at
        row = lax.broadcasted_iota(jnp.int32, (EXTRA, TILE), 0)
        ok = (slot >= first) & (slot < limit) & (row == 0)
        pack[to + dim : to + dim + EXTRA, :] = jnp.where(ok, 1.0, 0.0).astype(BF16)
    for copy in copies:
        copy.wait()
    to = base + rows // TILE * (dim + EXTRA)
    odd = lax.rem(me, 2) == 1
    own = nvbuf[...].astype(F32)
    none = jnp.zeros_like(own)
    both = [jnp.where(odd, none, own), jnp.where(odd, own, none), jnp.zeros((TILE - 2 * new, dim), F32)]
    pack[to : to + dim, :] = jnp.concatenate(both, axis=0).T.astype(BF16)
    row = lax.broadcasted_iota(jnp.int32, (EXTRA, TILE), 0)
    column = lax.broadcasted_iota(jnp.int32, (EXTRA, TILE), 1)
    mine = lax.div(column, new) == lax.rem(me, 2)
    pack[to + dim : to + dim + EXTRA, :] = jnp.where((row == 0) & mine, 1.0, 0.0).astype(BF16)


def fresh_mask(me, token, spans, new):
    key = lax.broadcasted_iota(jnp.int32, (2 * new, token.shape[1]), 0) + (me - lax.rem(me, 2)) * new
    ok = key <= token
    for k in range(spans.shape[1]):
        lo, hi = spans[0, k], spans[1, k]
        ok = ok | ((token >= lo) & (token < hi) & (key >= lo) & (key < hi))
    return ok


def attend_kernel(where, away, cache_dev, new, group, scale2, spans, own, other, q_ref, out, s0, s1, fresh_k, fresh_v):
    members, part, dim = q_ref.shape
    pair = WIDE // part
    n, rows = members // pair, WIDE
    me = where()
    core = lax.rem(me, 2)
    quad = (me - lax.rem(me, 2 * members)) ^ (2 * members if away else 0)
    base = cache_dev + new
    tall = dim + EXTRA
    s_refs = (s0, s1)

    odd = core == 1
    mine, theirs = own[cache_dev:base, :].astype(F32), other[cache_dev:base, :].astype(F32)
    fresh_k[0:new, :] = jnp.where(odd, theirs, mine).astype(BF16)
    fresh_k[new : 2 * new, :] = jnp.where(odd, mine, theirs).astype(BF16)
    at = base + cache_dev // TILE * tall
    fresh_v[...] = (own[at : at + tall, :].astype(F32) + other[at : at + tall, :].astype(F32)).astype(BF16)

    tiles = [(which, at) for which in (0, 1) for at in range(0, cache_dev, CHUNK)] + [None]

    def block(b):
        return q_ref[pair * b : pair * (b + 1)].reshape(rows, dim)

    def scores(b, tile, peak):
        if tile is None:
            s = lax.dot_general(fresh_k[...], block(b), NT, preferred_element_type=F32)
            lane = lax.broadcasted_iota(jnp.int32, (1, rows), 1)
            owner = quad + (pair * b + lax.div(lane, part)) * 2 + core
            token = owner * new + lax.div(lax.rem(lane, part), group)
            s = jnp.where(fresh_mask(me, token, spans, new), s, HIDDEN)
            to, size = 2 * cache_dev, 2 * new
        else:
            which, at = tile
            s = lax.dot_general((own, other)[which][at : at + CHUNK, :], block(b), NT, preferred_element_type=F32)
            to, size = which * cache_dev + at, CHUNK
        s_refs[b % 2][to : to + size, :] = s
        top = jnp.max(s.reshape(size // 8, 8, rows), axis=0)
        return top if peak is None else jnp.maximum(peak, top)

    def weigh(b, tile, peak, acc):
        if tile is None:
            s = s_refs[b % 2][2 * cache_dev : 2 * cache_dev + 2 * new, :]
            p = jnp.exp2((s - peak) * scale2)
            p = jnp.concatenate([p, jnp.zeros((TILE - 2 * new, rows), F32)], axis=0).astype(BF16)
            v = fresh_v[...]
        else:
            which, at = tile
            to = which * cache_dev + at
            p = jnp.exp2((s_refs[b % 2][to : to + CHUNK, :] - peak) * scale2).astype(BF16)
            starts = [base + (at // TILE + j) * tall for j in range(CHUNK // TILE)]
            v = jnp.concatenate([(own, other)[which][i : i + tall, :] for i in starts], axis=1)
        o = jnp.dot(v, p, preferred_element_type=F32)
        return o if acc is None else acc + o

    peak = None
    for tile in tiles:
        peak = scores(0, tile, peak)
    for b in range(n):
        top = jnp.max(peak, axis=0, keepdims=True)
        acc, peak = None, None
        for tile in tiles:
            acc = weigh(b, tile, top, acc)
            if b + 1 < n:
                peak = scores(b + 1, tile, peak)
        for j in range(pair):
            cut = slice(j * part, (j + 1) * part)
            write_message(out.at[pair * b + j], acc[0:dim, cut], top[:, cut] * scale2, acc[dim : dim + 1, cut])


def spread_kernel(q, _, out):
    for j in range(out.shape[0]):
        out[j] = q[...]


def merge_kernel(got, _, out, kept):
    write_message(out, *merge([got.at[j] for j in range(got.shape[0])]))


def final_kernel(got, back, out):
    numer, _, total = merge([got.at[j] for j in range(got.shape[0])] + [back])
    out[...] = (numer / total).T.astype(BF16)


def on_device(queries, new_keys, new_values, cache_k, cache_v, span_bounds, cache_len, doc_start):
    far, near, cores = (lax.axis_size(name) for name in ("far", "near", "core"))
    new, _, group, dim = queries.shape
    rows = new * group
    cache_dev = cache_k.shape[1]
    packed = cache_dev + new + (cache_dev // TILE + 1) * (dim + EXTRA)
    scale2 = math.log2(math.e) / math.sqrt(dim)

    def where():
        return (lax.axis_index("far") * near + lax.axis_index("near")) * cores + lax.axis_index("core")

    def across(x, axis):
        return lax.ppermute(x, axis, [(0, 1), (1, 0)])

    def quad(x):
        return lax.all_to_all(x, "near", split_axis=0, concat_axis=0, tiled=True)

    hbm = pl.BlockSpec(memory_space=pltpu.HBM)
    vmem = pl.BlockSpec(memory_space=pltpu.VMEM)
    smem = pl.BlockSpec(memory_space=pltpu.SMEM)
    params = pltpu.CompilerParams(vmem_limit_bytes=40 * 1024 * 1024)
    message = jax.ShapeDtypeStruct((dim + EXTRA, rows), BF16)
    dma = pltpu.SemaphoreType.DMA

    q = queries.reshape(rows, dim)
    q_far = across(q, "far")
    own = pl.pallas_call(
        functools.partial(pack_kernel, far * near * cores, where),
        out_shape=jax.ShapeDtypeStruct((packed, dim), BF16),
        in_specs=[hbm] * 4 + [smem] * 2,
        out_specs=vmem,
        scratch_shapes=[
            pltpu.VMEM((cache_dev, dim), BF16),
            pltpu.VMEM((cache_dev, dim), BF16),
            pltpu.VMEM((new, dim), BF16),
            dma,
            dma,
            dma((2,)),
        ],
        compiler_params=params,
        name="pack",
    )(cache_k, cache_v, new_keys.reshape(new, dim), new_values.reshape(new, dim), cache_len, doc_start)
    def spread(block, before, name):
        return pl.pallas_call(
            spread_kernel,
            out_shape=jax.ShapeDtypeStruct((near, rows, dim), BF16),
            in_specs=[vmem, pl.BlockSpec(memory_space=pl.ANY)],
            out_specs=vmem,
            compiler_params=params,
            name=name,
        )(block, before)

    q_far = spread(q_far, own, "spread_far")
    q_near = spread(q, q_far, "spread_near")
    q_far = quad(q_far)
    other = across(own, "core")
    q_near = quad(q_near)

    spans = span_bounds.T
    cost = pl.CostEstimate(
        flops=4 * near * rows * 2 * cache_dev * dim,
        bytes_accessed=4 << 20,
        transcendentals=near * rows * 2 * cache_dev,
    )

    def attend(blocks, away, name):
        return pl.pallas_call(
            functools.partial(attend_kernel, where, away, cache_dev, new, group, scale2),
            out_shape=jax.ShapeDtypeStruct((near,) + message.shape, BF16),
            in_specs=[smem] + [vmem] * 3,
            out_specs=vmem,
            scratch_shapes=[pltpu.VMEM((2 * cache_dev + 2 * new, WIDE), F32)] * 2
            + [pltpu.VMEM((2 * new, dim), BF16), pltpu.VMEM((dim + EXTRA, TILE), BF16)],
            compiler_params=params,
            cost_estimate=cost,
            name=name,
        )(spans, own, other, blocks)

    far_out = attend(q_far, True, "far_blocks")
    far_got = quad(far_out)
    near_out = attend(q_near, False, "near_blocks")
    anywhere = pl.BlockSpec(memory_space=pl.ANY)
    far_sum, near_out = pl.pallas_call(
        merge_kernel,
        out_shape=[message, jax.ShapeDtypeStruct(near_out.shape, BF16)],
        in_specs=[vmem, anywhere],
        out_specs=[vmem, anywhere],
        input_output_aliases={1: 1},
        compiler_params=params,
        name="merge_far",
    )(far_got, near_out)
    back = across(far_sum, "far")
    near_got = quad(near_out)
    result = pl.pallas_call(
        final_kernel,
        out_shape=jax.ShapeDtypeStruct((rows, dim), BF16),
        in_specs=[vmem] * 2,
        out_specs=vmem,
        compiler_params=params,
        name="merge_all",
    )(near_got, back)
    return result.reshape(new, 1, group, dim)


def solution(mesh):
    ctx, kvh, sess = (mesh.shape[name] for name in ("ctx", "kvh", "sess"))
    devices = mesh.devices.reshape(2, ctx // 4, 2, kvh, sess)
    split = Mesh(devices, ("far", "near", "core", "kvh", "sess"))
    ctx = ("far", "near", "core")
    return jax.shard_map(
        on_device,
        mesh=split,
        in_specs=(
            P(("sess",) + ctx, "kvh", None, None),
            P(("sess",) + ctx, "kvh", None),
            P(("sess",) + ctx, "kvh", None),
            P(("sess", "kvh"), ctx, None),
            P(("sess", "kvh"), ctx, None),
            P("sess", None),
            P("sess"),
            P("sess"),
        ),
        out_specs=P(("sess",) + ctx, "kvh", None, None),
        check_vma=False,
    )
```
